128 devices in a mesh: node: 8 (over x, core), dev: 16 (over y, z).
Axes of the slice: x: 4, y: 4, z: 4, core: 2. Of those that a mesh axis runs over, the one named last changes fastest.
Arguments:
- q_nope: bfloat16 [4096, 4096], P('node', 'dev'), may hold values from -6 to 6
- q_rope: bfloat16 [4096, 2048], P('node', 'dev'), may hold values from -75 to 75
- kv_latent: bfloat16 [4096, 512], P('node'), may hold values from -6 to 6
- k_rope: bfloat16 [4096, 64], P('node'), may hold values from -5 to 5
- pool_latent: bfloat16 [256, 128, 512], P(('node', 'dev')), may hold values from -12 to 12
- pool_rope: bfloat16 [256, 128, 64], P(('node', 'dev')), may hold values from -6 to 6
- block_table: int32 [4], replicated, may hold values from 0 to 255, as said below
- absorb_k: bfloat16 [32, 128, 512], P('dev'), may hold values from -0.5 to 0.5
- absorb_v: bfloat16 [32, 512, 128], P('dev'), may hold values from -1 to 1
- out_proj: bfloat16 [4096, 3584], P('dev'), may hold values from -0.375 to 0.375
- residual: bfloat16 [4096, 3584], P(('node', 'dev')), may hold values from -45 to 45
- norm_gain: bfloat16 [3584], replicated, may hold values from 0.25 to 1.75
- router: bfloat16 [3584, 64], replicated, may hold values from -0.09375 to 0.09375
- expert_ids: int32 [4096, 8], P(('node', 'dev')), may hold values from 0 to 63, all different within a row; in each aligned block of 32 rows (0 to 31, 32 to 63, ...) at most 8 rows name the same one
- expert_gate: bfloat16 [128, 3584, 512], P(('node', 'dev')), may hold values from -0.09375 to 0.09375
- expert_up: bfloat16 [128, 3584, 512], P(('node', 'dev')), may hold values from -0.09375 to 0.09375
- expert_down: bfloat16 [128, 512, 3584], P(('node', 'dev')), may hold values from -0.1875 to 0.1875
Outputs:
- attended: bfloat16 [4096, 3584], P(('node', 'dev'))
- expert_out: bfloat16 [4096, 3584], P(('node', 'dev'))
The draws below stay inside these ranges and needn't reach their ends.
Inputs may be any that keep to these rules, and one draw needn't show every extreme that they name: `block_table`: distinct pool block numbers. `expert_ids`: each row names 8 different experts. In the rows of one device no expert is named more than 8 times, a bound that some block reaches.
All inputs are finite; a program needn't handle non-finite values.
Results may differ from the reference program's by a relative error of at most 0.039.
Values may be sent and summed in bfloat16 or wider, within the bound.
No kernel may reach another device: no remote copies, remote signals or barrier semaphores. Data moves between devices by JAX's collectives and lax.ppermute only.
A program may use at most 128 MiB of HBM per device.

```python
import math
import jax
import jax.numpy as jnp
import numpy as np
from jax import lax

D = 3584
H = 32
NOPE = 128
ROPE = 64
KV = 512
VDIM = 128
F = 1024
SHARDS = 2
TOP = 8
BLOCK = 128
NB = 4
TOK_DEV = 32
HD = 2
F_SHARD = 512
EXP_NODE = 8
EXPERTS = 64
SPAN_NODE = 512
SPAN = 4096
POOL = 256
CAP = 8
N_NODE = 8
N_DEV = 16
DEVICES = 128


def draw_k_rope(key, part):
    key = jax.random.fold_in(key, 1)
    base_draw = jnp.clip(jax.random.normal(key, (SPAN, ROPE), jnp.float32), -5.0, 5.0)
    return base_draw.astype(jnp.bfloat16)


def draw_q_rope(key, part):
    key = jax.random.fold_in(key, 2)
    base_draw = jnp.clip(jax.random.normal(key, (SPAN, H * ROPE), jnp.float32), -5.0, 5.0)
    return base_draw.astype(jnp.bfloat16)


def draw_residual(key, part):
    key = jax.random.fold_in(key, 3)
    value_key, row_key, column_key = jax.random.split(key, 3)
    base_draw = jnp.clip(jax.random.normal(value_key, (SPAN, D), jnp.float32), -5.0, 5.0)
    lowest, highest = (0.3, 3.0)
    row_scale = jnp.exp(jax.random.uniform(row_key, (SPAN, 1), jnp.float32, math.log(lowest), math.log(highest)))
    column_scale = jnp.exp(jax.random.uniform(column_key, (1, D), jnp.float32, math.log(lowest), math.log(highest)))
    return (base_draw * row_scale * column_scale).astype(jnp.bfloat16)


def draw_block_table(key, part):
    key = jax.random.fold_in(key, 4)
    pick_key, order_key = jax.random.split(key)
    inner = jax.random.permutation(pick_key, POOL - 2)[:NB - 2].astype(jnp.int32) + 1
    chosen = jnp.concatenate([inner, jnp.array([0, POOL - 1], jnp.int32)])
    return jax.random.permutation(order_key, chosen).astype(jnp.int32)


def levels(own_key, dims, cuts, low, top_value):
    level, own = 1.0, jax.random.fold_in(own_key, 6)
    for axis_at, blocks in cuts:
        draws = jnp.exp(jax.random.uniform(jax.random.fold_in(own, axis_at), (blocks,), jnp.float32, low / len(cuts), top_value / len(cuts)))
        level = level * jnp.repeat(draws, dims[axis_at] // blocks).reshape([-1 if axis == axis_at else 1 for axis in range(len(dims))])
    return level


def deal_out(stream_key, own, number, rows, count, top, bound, skew):
    sequence = jax.random.permutation(stream_key, count)
    heavy_load, ordinary = load_shares(count, rows * top, bound, skew, True), load_shares(count, rows * top, bound, skew, False)
    places = jnp.arange(count)

    def named(sizes, rotation):
        used = int((sizes > 0).sum())
        fixed = max(1, used // 4)
        shifted = fixed + (places - fixed + rotation * (used - fixed)) % max(1, count - fixed)
        return jnp.zeros((count,), jnp.int32).at[sequence[jnp.where(places < fixed, places, shifted)]].set(jnp.asarray(sizes, jnp.int32))

    sizes = jnp.where(number % 4 == 0, named(heavy_load, number // 4), named(ordinary, number - number // 4 - 1))
    mixed = jax.random.permutation(jax.random.fold_in(own, 3), count)
    giver, taker = mixed[0:count // 2 * 2:2], mixed[1:count // 2 * 2:2]
    slack = jnp.minimum(sizes[giver] - 1, bound - sizes[taker]) // 2
    slack = jnp.where((giver == sequence[0]) | (taker == sequence[0]) | (sizes[taker] == 0), 0, jnp.maximum(slack, 0))
    shifted = jax.random.randint(jax.random.fold_in(own, 4), (count // 2,), 0, 1 << 20) % (slack + 1)
    sizes = sizes.at[giver].add(-shifted).at[taker].add(shifted)
    labels = jnp.searchsorted(jnp.cumsum(sizes), jnp.arange(rows * top), side="right").astype(jnp.int32)
    table = labels.reshape(top, rows).T
    table = table[jax.random.permutation(jax.random.fold_in(own, 1), rows)]
    rotation = jax.random.randint(jax.random.fold_in(own, 2), (rows, 1), 0, top)
    return jnp.take_along_axis(table, (jnp.arange(top)[None, :] + rotation) % top, axis=1)


def load_shares(amount, total, most, lean, full):
    loads = [(1 << 20) // math.isqrt(grade ** lean) + 1 for grade in range(1, amount + 1)]
    largest = most if full else min(most, max(-(-total // amount), total * loads[0] // sum(loads)))
    least = 1 if total - largest >= amount - 1 else 0
    given, surplus = [largest] + [least] * (amount - 1), total - largest - least * (amount - 1)
    while surplus > 0:
        candidates = [i for i in range(1, amount) if given[i] < largest] or [i for i in range(1, amount) if given[i] < most]
        whole, budget = sum([loads[i] for i in candidates]), surplus
        for i in candidates:
            extra = min(most - given[i], max(1, budget * loads[i] // whole), surplus)
            given[i] = given[i] + extra
            surplus = surplus - extra
    return np.array(given)


def noise(own_key, extent, spread, limit, pieces=(), kind=jnp.bfloat16):
    result = spread * jax.random.normal(own_key, extent, jnp.float32)
    if pieces:
        result = result * levels(own_key, extent, pieces, -0.22, 0.18)
    return jnp.clip(result, -limit, limit).astype(kind)


def setup_inputs(seed: int = 0) -> dict:
    splits = jax.random.split(jax.random.key(seed), 18)
    q_nope = noise(splits[0], (SPAN, H * NOPE), 1.0, 6.0, ((0, 8), (1, 16)))
    q_rope = draw_q_rope(jax.random.fold_in(splits[17], 71), 0)
    kv_latent = noise(splits[2], (SPAN, KV), 1.0, 6.0, ((0, 8),))
    k_rope = draw_k_rope(jax.random.fold_in(splits[17], 71), 0)
    pool_latent = noise(splits[4], (POOL, BLOCK, KV), 2.0, 12.0, ((0, 128),))
    pool_rope = noise(splits[5], (POOL, BLOCK, ROPE), 1.0, 6.0, ((0, 128),))
    block_table = draw_block_table(jax.random.fold_in(splits[17], 71), 0)
    absorb_k = noise(splits[7], (H, NOPE, KV), NOPE ** -0.5, 0.5, ((0, 16),))
    absorb_v = noise(splits[8], (H, KV, VDIM), 32 ** -0.5, 1.0, ((0, 16),))
    out_proj = noise(splits[9], (H * VDIM, D), 256 ** -0.5, 0.375, ((0, 16),))
    residual = draw_residual(jax.random.fold_in(splits[17], 71), 0)
    norm_gain = jnp.clip(1.0 + 0.15 * jax.random.normal(splits[11], (D,), jnp.float32), 0.25, 1.75).astype(jnp.bfloat16)
    router = noise(splits[12], (D, EXPERTS), D ** -0.5, 0.09375)
    expert_ids_keys = jax.random.split(jax.random.fold_in(splits[13], 1), SPAN // TOK_DEV)
    expert_ids_turns = jax.random.permutation(jax.random.fold_in(splits[13], 3), SPAN // TOK_DEV)
    expert_ids = jax.vmap(lambda own, number: deal_out(jax.random.fold_in(splits[13], 2), own, number, TOK_DEV, EXPERTS, TOP, CAP, 2))(expert_ids_keys, expert_ids_turns).reshape((SPAN, TOP))
    expert_gate = noise(splits[14], (EXPERTS * SHARDS, D, F_SHARD), D ** -0.5, 0.09375, ((0, 128),))
    expert_up = noise(splits[15], (EXPERTS * SHARDS, D, F_SHARD), D ** -0.5, 0.09375, ((0, 128),))
    expert_down = noise(splits[16], (EXPERTS * SHARDS, F_SHARD, D), F ** -0.5, 0.1875, ((0, 128),))
    return dict(q_nope=q_nope, q_rope=q_rope, kv_latent=kv_latent, k_rope=k_rope, pool_latent=pool_latent, pool_rope=pool_rope, block_table=block_table, absorb_k=absorb_k, absorb_v=absorb_v, out_proj=out_proj, residual=residual, norm_gain=norm_gain, router=router, expert_ids=expert_ids, expert_gate=expert_gate, expert_up=expert_up, expert_down=expert_down)


ROUTE_SCALE = 2.827
NORM_EPS = 1e-06
FAR_BELOW = -1e+30

def attend_group(q_lat, q_rot, keys_lat, keys_rot, visible, softmax_scale):
    scores = (jnp.dot(q_lat, keys_lat.T, preferred_element_type=jnp.float32) + jnp.dot(q_rot, keys_rot.T, preferred_element_type=jnp.float32)) * softmax_scale
    masked = jnp.where(visible, scores, FAR_BELOW)
    row_top = lax.optimization_barrier(jnp.max(masked, axis=1, keepdims=True))
    exp_scores = jnp.where(visible, jnp.exp(masked - row_top), 0.0)
    row_sum = lax.optimization_barrier(jnp.sum(exp_scores, axis=1, keepdims=True))
    mixed = jnp.dot(exp_scores.astype(jnp.bfloat16), keys_lat, preferred_element_type=jnp.float32)
    return (mixed / row_sum).astype(jnp.bfloat16)

def reference(q_nope, q_rope, kv_latent, k_rope, pool_latent, pool_rope, block_table, absorb_k, absorb_v, out_proj, residual, norm_gain, router, expert_ids, expert_gate, expert_up, expert_down):
    softmax_scale = 1.0 / math.sqrt(NOPE + ROPE)
    prefix_lat = pool_latent[block_table].reshape(NB * BLOCK, KV)
    prefix_rot = pool_rope[block_table].reshape(NB * BLOCK, ROPE)
    nope_split = q_nope.reshape(N_NODE, SPAN_NODE, N_DEV, HD, NOPE)
    rope_split = q_rope.reshape(N_NODE, SPAN_NODE, N_DEV, HD, ROPE)
    absorb_keys = absorb_k.reshape(N_DEV, HD, NOPE, KV)
    absorb_values = absorb_v.reshape(N_DEV, HD, KV, VDIM)
    proj_groups = out_proj.reshape(N_DEV, HD * VDIM, D)
    node_blocks = []
    for node_index in range(N_NODE):
        seen_rows = (node_index + 1) * SPAN_NODE
        keys_lat = jnp.concatenate([prefix_lat, kv_latent[:seen_rows]], 0)
        keys_rot = jnp.concatenate([prefix_rot, k_rope[:seen_rows]], 0)
        key_pos = jnp.concatenate([jnp.full((NB * BLOCK,), -1, jnp.int32), jnp.arange(seen_rows, dtype=jnp.int32)])
        q_pos = node_index * SPAN_NODE + jnp.arange(SPAN_NODE * HD, dtype=jnp.int32) // HD
        visible = key_pos[None, :] <= q_pos[:, None]
        q_node = nope_split[node_index]
        rot_node = rope_split[node_index]

        def add_group(head_group, acc_sum):
            q_part = lax.dynamic_index_in_dim(q_node, head_group, 1, False)
            key_absorb = lax.dynamic_index_in_dim(absorb_keys, head_group, 0, False)
            q_lat = jnp.einsum('qhn,hnc->qhc', q_part.astype(jnp.float32), key_absorb.astype(jnp.float32))
            q_lat = q_lat.astype(jnp.bfloat16).reshape(SPAN_NODE * HD, KV)
            q_rot = lax.dynamic_index_in_dim(rot_node, head_group, 1, False).reshape(SPAN_NODE * HD, ROPE)
            head_lat = attend_group(q_lat, q_rot, keys_lat, keys_rot, visible, softmax_scale).reshape(SPAN_NODE, HD, KV)
            value_absorb = lax.dynamic_index_in_dim(absorb_values, head_group, 0, False)
            head_out = jnp.einsum('qhc,hcv->qhv', head_lat.astype(jnp.float32), value_absorb.astype(jnp.float32))
            head_out = head_out.astype(jnp.bfloat16).reshape(SPAN_NODE, HD * VDIM)
            out_rows = lax.dynamic_index_in_dim(proj_groups, head_group, 0, False)
            group_term = jnp.dot(head_out, out_rows, preferred_element_type=jnp.float32).astype(jnp.bfloat16)
            group_term = lax.optimization_barrier(group_term)
            return acc_sum + group_term.astype(jnp.float32)
        node_blocks.append(lax.fori_loop(0, N_DEV, add_group, jnp.zeros((SPAN_NODE, D), jnp.float32)))
    attn_sum = jnp.concatenate(node_blocks, 0)
    attended = (residual.astype(jnp.float32) + attn_sum).astype(jnp.bfloat16)
    stream = attended.astype(jnp.float32)
    normed = stream * lax.rsqrt(lax.optimization_barrier(jnp.mean(stream * stream, axis=1, keepdims=True)) + NORM_EPS)
    normed = (normed * norm_gain.astype(jnp.float32)).astype(jnp.bfloat16)
    logits = jnp.dot(normed, router, preferred_element_type=jnp.float32)
    picked = jnp.take_along_axis(logits, expert_ids, axis=1)
    gates = jax.nn.sigmoid(picked)
    weights = (ROUTE_SCALE * gates / lax.optimization_barrier(jnp.sum(gates, axis=1, keepdims=True))).astype(jnp.bfloat16)
    weights = lax.optimization_barrier(weights).astype(jnp.float32)
    routed_hit = expert_ids[:, :, None] == jnp.arange(EXPERTS, dtype=jnp.int32)[None, None, :]
    is_used = jnp.any(routed_hit, axis=1).astype(jnp.int32)
    pair_weight = lax.optimization_barrier(jnp.sum(jnp.where(routed_hit, weights[:, :, None], 0.0), axis=1))
    used_blocks = is_used.reshape(DEVICES, TOK_DEV, EXPERTS)
    slot_rank = jnp.cumsum(used_blocks, axis=1) - used_blocks
    slot_ids = jnp.arange(CAP, dtype=jnp.int32)
    slot_hit = (used_blocks[..., None] == 1) & (slot_rank[..., None] == slot_ids[None, None, None, :])
    hit_count = slot_hit.astype(jnp.int32)
    token_numbers = jnp.arange(SPAN, dtype=jnp.int32).reshape(DEVICES, TOK_DEV)
    token_at = lax.optimization_barrier(jnp.sum(hit_count * token_numbers[:, :, None, None], axis=1))
    live_slot = lax.optimization_barrier(jnp.sum(hit_count, axis=1))
    slot_weight = lax.optimization_barrier(jnp.sum(jnp.where(slot_hit, pair_weight.reshape(DEVICES, TOK_DEV, EXPERTS)[..., None], 0.0), axis=1))
    token_at = jnp.transpose(token_at, (1, 0, 2)).reshape(N_NODE, EXP_NODE, DEVICES * CAP)
    live_slot = jnp.transpose(live_slot, (1, 0, 2)).reshape(N_NODE, EXP_NODE, DEVICES * CAP)
    slot_weight = jnp.transpose(slot_weight, (1, 0, 2)).reshape(N_NODE, EXP_NODE, DEVICES * CAP)

    def add_expert(out_total, inputs):
        expert_index, rows_at, live_here, weight_here = inputs
        token_rows = jnp.where(live_here[:, None] == 1, normed[rows_at], jnp.zeros((), jnp.bfloat16))
        expert_sum = jnp.zeros((DEVICES * CAP, D), jnp.float32)
        for shard_index in range(SHARDS):
            row_index = expert_index * SHARDS + shard_index
            gate_rows = lax.dynamic_index_in_dim(expert_gate, row_index, 0, False)
            up_rows = lax.dynamic_index_in_dim(expert_up, row_index, 0, False)
            down_rows = lax.dynamic_index_in_dim(expert_down, row_index, 0, False)
            gate_act = jnp.dot(token_rows, gate_rows, preferred_element_type=jnp.float32)
            up_act = jnp.dot(token_rows, up_rows, preferred_element_type=jnp.float32)
            hidden = (jax.nn.silu(gate_act) * up_act).astype(jnp.bfloat16)
            part_out = jnp.dot(hidden, down_rows, preferred_element_type=jnp.float32).astype(jnp.bfloat16)
            part_out = lax.optimization_barrier(part_out)
            expert_sum = expert_sum + part_out.astype(jnp.float32)
        scaled = expert_sum * (weight_here * live_here.astype(jnp.float32))[:, None]
        return (out_total.at[rows_at].add(scaled), None)

    def add_node(grand_total, node_inputs):
        node_part, unused_part = lax.scan(add_expert, jnp.zeros((SPAN, D), jnp.float32), node_inputs)
        node_part = lax.optimization_barrier(node_part.astype(jnp.bfloat16))
        return (grand_total + node_part.astype(jnp.float32), None)
    expert_numbers = jnp.arange(EXPERTS, dtype=jnp.int32).reshape(N_NODE, EXP_NODE)
    out_total, unused_out = lax.scan(add_node, jnp.zeros((SPAN, D), jnp.float32), (expert_numbers, token_at, live_slot, slot_weight))
    return (attended, out_total.astype(jnp.bfloat16))
```

```python
import functools
import math

import jax
import jax.numpy as jnp
from jax import lax
from jax.experimental import pallas as pl
from jax.experimental.pallas import tpu as pltpu
from jax.sharding import PartitionSpec as P

ROUTE_SCALE = 2.827
NORM_EPS = 1e-06
FAR_BELOW = -1e30
ALL = ("node", "dev")
VMEM_BYTES = 60 * 1024 * 1024
F32 = jnp.float32
BF16 = jnp.bfloat16


def dot(a, b, dims=(((1,), (0,)), ((), ()))):
    return lax.dot_general(a, b, dims, preferred_element_type=F32)


def swap(value, axis):
    return lax.all_to_all(value, axis, split_axis=0, concat_axis=0, tiled=True)


def attention_kernel(
    q_nope, q_rope, keys, prefix, absorb_k, absorb_v, out_proj, terms, q_lat, top, total, mixed
):
    heads, nope, rank = absorb_k.shape
    tokens = q_nope.shape[0]
    rope = q_rope.shape[1] // heads
    block = prefix.shape[0]
    span = block - rope
    scale = 1.0 / math.sqrt(nope + rope)
    node = lax.axis_index("node")
    first = pl.program_id(0) * tokens

    for h in range(heads):
        part = dot(q_nope[:, h * nope : (h + 1) * nope], absorb_k[h])
        q_lat[h * tokens : (h + 1) * tokens] = part.astype(BF16)

    def fold(lat, rot, mask, fresh):
        for h in range(heads):
            rows = pl.ds(h * tokens, tokens)
            scores = dot(q_lat[rows], lat, (((1,), (1,)), ((), ())))
            scores = scores + dot(q_rope[:, h * rope : (h + 1) * rope], rot)
            if mask is not None:
                scores = jnp.where(mask, scores, FAR_BELOW)
            row_top = jnp.max(scores, axis=1, keepdims=True)
            if not fresh:
                row_top = jnp.maximum(row_top, top[rows])
            exp_scores = jnp.exp((scores - row_top) * scale)
            row_sum = jnp.sum(exp_scores, axis=1, keepdims=True)
            mix = dot(exp_scores.astype(BF16), lat)
            if not fresh:
                shrink = jnp.exp((top[rows] - row_top) * scale)
                row_sum = row_sum + total[rows] * shrink
                mix = mix + mixed[rows] * shrink
            top[rows] = row_top
            total[rows] = row_sum
            mixed[rows] = mix

    fold(prefix[:span], prefix[span:], None, True)

    def earlier(j, carry):
        at = pl.multiple_of(j * block, 64)
        fold(keys[pl.ds(at, span)], keys[pl.ds(at + span, rope)], None, False)
        return carry

    lax.fori_loop(0, node, earlier, 0)
    at = pl.multiple_of(node * block, 64)
    q_pos = first + lax.broadcasted_iota(jnp.int32, (tokens, span), 0)
    key_pos = lax.broadcasted_iota(jnp.int32, (tokens, span), 1)
    fold(keys[pl.ds(at, span)], keys[pl.ds(at + span, rope)], key_pos <= q_pos, False)

    outs = []
    for h in range(heads):
        rows = pl.ds(h * tokens, tokens)
        head_lat = (mixed[rows] / total[rows]).astype(BF16)
        outs.append(dot(head_lat, absorb_v[h]).astype(BF16))
    head_out = jnp.concatenate(outs, axis=1)
    width = out_proj.shape[1]
    step = 512
    for c in range(0, width, step):
        terms[:, c : c + step] = dot(head_out, out_proj[:, c : c + step]).astype(BF16)


def attention(q_nope, q_rope, keys, prefix, absorb_k, absorb_v, out_proj):
    rows = q_nope.shape[0]
    tile = min(256, rows)
    heads, nope, rank = absorb_k.shape
    width = out_proj.shape[1]
    whole = pl.BlockSpec(memory_space=pltpu.VMEM)
    return pl.pallas_call(
        attention_kernel,
        grid=(rows // tile,),
        out_shape=jax.ShapeDtypeStruct((rows, width), BF16),
        in_specs=[
            pl.BlockSpec((tile, q_nope.shape[1]), lambda i: (i, 0)),
            pl.BlockSpec((tile, q_rope.shape[1]), lambda i: (i, 0)),
            whole,
            whole,
            whole,
            whole,
            whole,
        ],
        out_specs=pl.BlockSpec((tile, width), lambda i: (i, 0)),
        scratch_shapes=[
            pltpu.VMEM((heads * tile, rank), BF16),
            pltpu.VMEM((heads * tile, 1), F32),
            pltpu.VMEM((heads * tile, 1), F32),
            pltpu.VMEM((heads * tile, rank), F32),
        ],
        compiler_params=pltpu.CompilerParams(vmem_limit_bytes=VMEM_BYTES),
        name="attention",
    )(q_nope, q_rope, keys, prefix, absorb_k, absorb_v, out_proj)


def route_kernel(terms, residual, gain, router, ids, attended, outgoing, shares, *, shards, cap):
    groups, tokens, width = terms.shape
    experts = router.shape[1]
    top_k = ids.shape[1]
    acc = terms[0].astype(F32)
    for g in range(1, groups):
        acc = acc + terms[g].astype(F32)
    stream = (residual[...].astype(F32) + acc).astype(BF16)
    attended[...] = stream
    stream = stream.astype(F32)
    mean = jnp.mean(stream * stream, axis=1, keepdims=True)
    normed = (stream * lax.rsqrt(mean + NORM_EPS) * gain[...].astype(F32)).astype(BF16)
    logits = dot(normed, router[...])
    expert = lax.broadcasted_iota(jnp.int32, (tokens, experts), 1)
    hits = [ids[:, j : j + 1] == expert for j in range(top_k)]
    gates = [
        jax.nn.sigmoid(jnp.sum(jnp.where(hit, logits, 0.0), axis=1, keepdims=True)) for hit in hits
    ]
    gate_sum = functools.reduce(lambda a, b: a + b, gates)
    weight = jnp.zeros((tokens, experts), F32)
    used = jnp.zeros((tokens, experts), F32)
    for hit, gate in zip(hits, gates):
        weight = jnp.where(hit, ROUTE_SCALE * gate / gate_sum, weight)
        used = jnp.where(hit, 1.0, used)
    weight = weight.astype(BF16)
    used = used.astype(BF16)
    below = lax.broadcasted_iota(jnp.int32, (tokens, tokens), 1) < lax.broadcasted_iota(
        jnp.int32, (tokens, tokens), 0
    )
    rank = dot(below.astype(BF16), used).astype(BF16)
    slots = experts * shards * cap
    owner = lax.broadcasted_iota(jnp.int32, (experts, slots), 1) // (shards * cap)
    spread = (owner == lax.broadcasted_iota(jnp.int32, (experts, slots), 0)).astype(BF16)
    slot = lax.broadcasted_iota(jnp.int32, (tokens, slots), 1) % cap
    filled = (dot(used, spread) > 0.5) & (dot(rank, spread) == slot.astype(F32))
    shares[...] = jnp.where(filled, dot(weight, spread), 0.0).astype(BF16)
    fill = filled.astype(F32).astype(BF16)
    step = 512
    for c in range(0, width, step):
        outgoing[:, c : c + step] = dot(
            fill, normed[:, c : c + step], (((0,), (0,)), ((), ()))
        ).astype(BF16)


def route(terms, residual, gain, router, ids, shards, cap):
    tokens, width = residual.shape
    slots = router.shape[1] * shards * cap
    whole = pl.BlockSpec(memory_space=pltpu.VMEM)
    return pl.pallas_call(
        functools.partial(route_kernel, shards=shards, cap=cap),
        out_shape=(
            jax.ShapeDtypeStruct((tokens, width), BF16),
            jax.ShapeDtypeStruct((slots, width), BF16),
            jax.ShapeDtypeStruct((tokens, slots), BF16),
        ),
        in_specs=[whole] * 5,
        out_specs=(whole, whole, whole),
        compiler_params=pltpu.CompilerParams(vmem_limit_bytes=VMEM_BYTES),
        name="route",
    )(terms, residual, gain, router, ids)


def expert_kernel(rows, gate, up, down, out):
    x = rows[...]
    gate_act = dot(x, gate[...])
    up_act = dot(x, up[...])
    hidden = (jax.nn.silu(gate_act) * up_act).astype(BF16)
    width = down.shape[1]
    step = 512
    for c in range(0, width, step):
        out[:, c : c + step] = dot(hidden, down[:, c : c + step]).astype(BF16)


def experts(rows, gate, up, down):
    count, width = rows.shape
    tile = min(256, count)
    whole = pl.BlockSpec(memory_space=pltpu.VMEM)
    return pl.pallas_call(
        expert_kernel,
        grid=(count // tile,),
        out_shape=jax.ShapeDtypeStruct((count, width), BF16),
        in_specs=[pl.BlockSpec((tile, width), lambda i: (i, 0)), whole, whole, whole],
        out_specs=pl.BlockSpec((tile, width), lambda i: (i, 0)),
        compiler_params=pltpu.CompilerParams(vmem_limit_bytes=VMEM_BYTES),
        name="experts",
    )(rows, gate, up, down)


def combine_kernel(shares, returned, out):
    out[...] = dot(shares[...], returned[...]).astype(BF16)


def combine(shares, returned):
    tokens, slots = shares.shape
    width = returned.shape[1]
    tile = 512
    return pl.pallas_call(
        combine_kernel,
        grid=(width // tile,),
        out_shape=jax.ShapeDtypeStruct((tokens, width), BF16),
        in_specs=[
            pl.BlockSpec((tokens, slots), lambda i: (0, 0)),
            pl.BlockSpec((slots, tile), lambda i: (0, i)),
        ],
        out_specs=pl.BlockSpec((tokens, tile), lambda i: (0, i)),
        compiler_params=pltpu.CompilerParams(vmem_limit_bytes=VMEM_BYTES),
        name="combine",
    )(shares, returned)


def listed_prefix(pool_latent, pool_rope, block_table, devices):
    held, block, rank = pool_latent.shape
    rope = pool_rope.shape[2]
    count = block_table.shape[0]
    me = lax.axis_index(ALL)
    mine = block_table // held == me
    slot = block_table % held
    lat = jnp.where(mine[:, None, None], pool_latent[slot], 0).astype(BF16)
    rot = jnp.where(mine[:, None, None], pool_rope[slot], 0).astype(BF16)
    lat = lat.reshape(count * block, rank)
    rot = jnp.transpose(rot, (2, 0, 1)).reshape(rope * count * block // rank, rank)
    both = jnp.concatenate([lat, rot], 0)
    parts = both.reshape(devices, -1, 128)
    arrived = swap(parts, ALL)
    piece = jnp.sum(arrived.astype(F32), axis=0).astype(BF16)
    return swap(jnp.broadcast_to(piece[None], parts.shape), ALL).reshape(both.shape)


def on_device(
    q_nope,
    q_rope,
    kv_latent,
    k_rope,
    pool_latent,
    pool_rope,
    block_table,
    absorb_k,
    absorb_v,
    out_proj,
    residual,
    norm_gain,
    router,
    expert_ids,
    expert_gate,
    expert_up,
    expert_down,
):
    node_count = lax.axis_size("node")
    dev_count = lax.axis_size("dev")
    devices = node_count * dev_count
    tokens, width = residual.shape
    expert_count = router.shape[1]
    shards = devices // expert_count
    cap = max(2, 2 * tokens * expert_ids.shape[1] // expert_count)

    keys_here = jnp.concatenate([kv_latent, k_rope.T], 0)
    keys = lax.all_gather(keys_here, "node", axis=0, tiled=True)
    prefix = listed_prefix(pool_latent, pool_rope, block_table, devices)

    terms = attention(q_nope, q_rope, keys, prefix, absorb_k, absorb_v, out_proj)
    terms = swap(terms.reshape(dev_count, tokens, width), "dev")
    attended, outgoing, shares = route(
        terms, residual, norm_gain.reshape(1, width), router, expert_ids, shards, cap
    )
    arrived = swap(outgoing.reshape(devices, cap, width), ALL)
    served = experts(
        arrived.reshape(devices * cap, width), expert_gate[0], expert_up[0], expert_down[0]
    )
    returned = swap(served.reshape(devices, cap, width), ALL)
    return attended, combine(shares, returned.reshape(devices * cap, width))


def solution(mesh):
    placed = (
        P("node", "dev"),
        P("node", "dev"),
        P("node", None),
        P("node", None),
        P(ALL, None, None),
        P(ALL, None, None),
        P(),
        P("dev", None, None),
        P("dev", None, None),
        P("dev", None),
        P(ALL, None),
        P(),
        P(),
        P(ALL, None),
        P(ALL, None, None),
        P(ALL, None, None),
        P(ALL, None, None),
    )
    return jax.shard_map(
        on_device,
        mesh=mesh,
        in_specs=placed,
        out_specs=(P(ALL, None), P(ALL, None)),
        check_vma=False,
    )
```

```python
import functools
import math

import jax
import jax.numpy as jnp
from jax import lax
from jax.experimental import pallas as pl
from jax.experimental.pallas import tpu as pltpu
from jax.sharding import PartitionSpec as P

ROUTE_SCALE = 2.827
NORM_EPS = 1e-06
FAR_BELOW = -1e30
ALL = ("node", "dev")
VMEM_BYTES = 60 * 1024 * 1024
F32 = jnp.float32
BF16 = jnp.bfloat16


def dot(a, b, dims=(((1,), (0,)), ((), ()))):
    return lax.dot_general(a, b, dims, preferred_element_type=F32)


def swap(value, axis):
    return lax.all_to_all(value, axis, split_axis=0, concat_axis=0, tiled=True)


def attention_kernel(
    q_nope, q_rope, keys, prefix, absorb_k, absorb_v, out_proj, terms, q_lat, top, total, mixed
):
    heads, nope, rank = absorb_k.shape
    tokens = q_nope.shape[0]
    rope = q_rope.shape[1] // heads
    block = prefix.shape[0]
    span = block - rope
    scale = 1.0 / math.sqrt(nope + rope)
    node = lax.axis_index("node")
    first = pl.program_id(0) * tokens

    for h in range(heads):
        part = dot(q_nope[:, h * nope : (h + 1) * nope], absorb_k[h])
        q_lat[h * tokens : (h + 1) * tokens] = part.astype(BF16)

    def fold(lat, rot, mask, fresh):
        for h in range(heads):
            rows = pl.ds(h * tokens, tokens)
            scores = dot(q_lat[rows], lat, (((1,), (1,)), ((), ())))
            scores = scores + dot(q_rope[:, h * rope : (h + 1) * rope], rot)
            if mask is not None:
                scores = jnp.where(mask, scores, FAR_BELOW)
            row_top = jnp.max(scores, axis=1, keepdims=True)
            if not fresh:
                row_top = jnp.maximum(row_top, top[rows])
            exp_scores = jnp.exp((scores - row_top) * scale)
            row_sum = jnp.sum(exp_scores, axis=1, keepdims=True)
            mix = dot(exp_scores.astype(BF16), lat)
            if not fresh:
                shrink = jnp.exp((top[rows] - row_top) * scale)
                row_sum = row_sum + total[rows] * shrink
                mix = mix + mixed[rows] * shrink
            top[rows] = row_top
            total[rows] = row_sum
            mixed[rows] = mix

    fold(prefix[:span], prefix[span:], None, True)

    def earlier(j, carry):
        at = pl.multiple_of(j * block, 64)
        fold(keys[pl.ds(at, span)], keys[pl.ds(at + span, rope)], None, False)
        return carry

    lax.fori_loop(0, node, earlier, 0)
    at = pl.multiple_of(node * block, 64)
    q_pos = first + lax.broadcasted_iota(jnp.int32, (tokens, span), 0)
    key_pos = lax.broadcasted_iota(jnp.int32, (tokens, span), 1)
    fold(keys[pl.ds(at, span)], keys[pl.ds(at + span, rope)], key_pos <= q_pos, False)

    outs = []
    for h in range(heads):
        rows = pl.ds(h * tokens, tokens)
        head_lat = (mixed[rows] / total[rows]).astype(BF16)
        outs.append(dot(head_lat, absorb_v[h]).astype(BF16))
    head_out = jnp.concatenate(outs, axis=1)
    width = out_proj.shape[1]
    step = 512
    for c in range(0, width, step):
        terms[:, c : c + step] = dot(head_out, out_proj[:, c : c + step]).astype(BF16)


def attention(q_nope, q_rope, keys, prefix, absorb_k, absorb_v, out_proj):
    rows = q_nope.shape[0]
    tile = min(256, rows)
    heads, nope, rank = absorb_k.shape
    width = out_proj.shape[1]
    whole = pl.BlockSpec(memory_space=pltpu.VMEM)
    return pl.pallas_call(
        attention_kernel,
        grid=(rows // tile,),
        out_shape=jax.ShapeDtypeStruct((rows, width), BF16),
        in_specs=[
            pl.BlockSpec((tile, q_nope.shape[1]), lambda i: (i, 0)),
            pl.BlockSpec((tile, q_rope.shape[1]), lambda i: (i, 0)),
            whole,
            whole,
            whole,
            whole,
            whole,
        ],
        out_specs=pl.BlockSpec((tile, width), lambda i: (i, 0)),
        scratch_shapes=[
            pltpu.VMEM((heads * tile, rank), BF16),
            pltpu.VMEM((heads * tile, 1), F32),
            pltpu.VMEM((heads * tile, 1), F32),
            pltpu.VMEM((heads * tile, rank), F32),
        ],
        compiler_params=pltpu.CompilerParams(vmem_limit_bytes=VMEM_BYTES),
        name="attention",
    )(q_nope, q_rope, keys, prefix, absorb_k, absorb_v, out_proj)


def slot_place(column, nodes, cap, experts):
    half = cap // 2
    devs = 2 * experts // nodes
    device, low = column // half, column % half
    node, dev = device // devs, device % devs
    expert = (experts // nodes) * (node // 2 * 2 + dev % 2) + dev // 2
    return expert, node % 2 * half + low


def route_kernel(terms, residual, gain, router, ids, attended, outgoing, shares, *, nodes, cap):
    groups, tokens, width = terms.shape
    experts = router.shape[1]
    top_k = ids.shape[1]
    acc = terms[0].astype(F32)
    for g in range(1, groups):
        acc = acc + terms[g].astype(F32)
    stream = (residual[...].astype(F32) + acc).astype(BF16)
    attended[...] = stream
    stream = stream.astype(F32)
    mean = jnp.mean(stream * stream, axis=1, keepdims=True)
    normed = (stream * lax.rsqrt(mean + NORM_EPS) * gain[...].astype(F32)).astype(BF16)
    logits = dot(normed, router[...])
    expert = lax.broadcasted_iota(jnp.int32, (tokens, experts), 1)
    hits = [ids[:, j : j + 1] == expert for j in range(top_k)]
    gates = [
        jax.nn.sigmoid(jnp.sum(jnp.where(hit, logits, 0.0), axis=1, keepdims=True)) for hit in hits
    ]
    gate_sum = functools.reduce(lambda a, b: a + b, gates)
    weight = jnp.zeros((tokens, experts), F32)
    used = jnp.zeros((tokens, experts), F32)
    for hit, gate in zip(hits, gates):
        weight = jnp.where(hit, ROUTE_SCALE * gate / gate_sum, weight)
        used = jnp.where(hit, 1.0, used)
    weight = weight.astype(BF16)
    used = used.astype(BF16)
    below = lax.broadcasted_iota(jnp.int32, (tokens, tokens), 1) < lax.broadcasted_iota(
        jnp.int32, (tokens, tokens), 0
    )
    rank = dot(below.astype(BF16), used).astype(BF16)
    slots = experts * cap
    owner, _ = slot_place(lax.broadcasted_iota(jnp.int32, (experts, slots), 1), nodes, cap, experts)
    spread = (owner == lax.broadcasted_iota(jnp.int32, (experts, slots), 0)).astype(BF16)
    _, slot = slot_place(lax.broadcasted_iota(jnp.int32, (tokens, slots), 1), nodes, cap, experts)
    filled = (dot(used, spread) > 0.5) & (dot(rank, spread) == slot.astype(F32))
    shares[...] = jnp.where(filled, dot(weight, spread), 0.0).astype(BF16)
    fill = filled.astype(F32).astype(BF16)
    step = 512
    for c in range(0, width, step):
        outgoing[:, c : c + step] = dot(
            fill, normed[:, c : c + step], (((0,), (0,)), ((), ()))
        ).astype(BF16)


def route(terms, residual, gain, router, ids, nodes, cap):
    tokens, width = residual.shape
    slots = router.shape[1] * cap
    whole = pl.BlockSpec(memory_space=pltpu.VMEM)
    return pl.pallas_call(
        functools.partial(route_kernel, nodes=nodes, cap=cap),
        out_shape=(
            jax.ShapeDtypeStruct((tokens, width), BF16),
            jax.ShapeDtypeStruct((slots, width), BF16),
            jax.ShapeDtypeStruct((tokens, slots), BF16),
        ),
        in_specs=[whole] * 5,
        out_specs=(whole, whole, whole),
        compiler_params=pltpu.CompilerParams(vmem_limit_bytes=VMEM_BYTES),
        name="route",
    )(terms, residual, gain, router, ids)


def expert_kernel(rows, *refs):
    sources, (out, gates, ups, downs, sems) = refs[:12], refs[12:]
    node, dev = lax.axis_index("node"), lax.axis_index("dev")
    keeper = node % 2 == dev % 2
    own, crossed, twin, twin_crossed = (sources[3 * i : 3 * i + 3] for i in range(4))
    slots = (gates, ups, downs)

    def copy(source, share, part):
        return pltpu.make_async_copy(
            source[part].at[0], slots[part].at[share], sems.at[share * 3 + part]
        )

    order = ((0, 0), (0, 1), (1, 0), (1, 1), (0, 2), (1, 2))

    @pl.when(keeper)
    def _():
        for share, part in order:
            copy((own, crossed)[share], share, part).start()

    @pl.when(jnp.logical_not(keeper))
    def _():
        for share, part in order:
            copy((twin, twin_crossed)[share], share, part).start()

    x = rows[...]
    hidden = []
    for share in range(2):
        copy(own, share, 0).wait()
        gate_act = dot(x, gates[share])
        copy(own, share, 1).wait()
        up_act = dot(x, ups[share])
        hidden.append((jax.nn.silu(gate_act) * up_act).astype(BF16))
    for share in range(2):
        copy(own, share, 2).wait()
    width = out.shape[1]
    step = 512
    for c in range(0, width, step):
        part = dot(hidden[0], downs[0, :, c : c + step])
        part = part + dot(hidden[1], downs[1, :, c : c + step])
        out[:, c : c + step] = part.astype(BF16)


def experts(rows, sources):
    count, width = rows.shape
    hidden = sources[0].shape[2]
    whole = pl.BlockSpec(memory_space=pltpu.VMEM)
    return pl.pallas_call(
        expert_kernel,
        out_shape=jax.ShapeDtypeStruct((count, width), BF16),
        in_specs=[whole] + [pl.BlockSpec(memory_space=pl.ANY)] * 12,
        out_specs=whole,
        scratch_shapes=[
            pltpu.VMEM((2, width, hidden), BF16),
            pltpu.VMEM((2, width, hidden), BF16),
            pltpu.VMEM((2, hidden, width), BF16),
            pltpu.SemaphoreType.DMA((6,)),
        ],
        compiler_params=pltpu.CompilerParams(vmem_limit_bytes=VMEM_BYTES),
        name="experts",
    )(rows, *sources)


def placed_weights(weights, nodes, devs):
    across, beside = [], []
    for node in range(nodes):
        for dev in range(devs):
            if node % 2 == dev % 2:
                across.append((node * devs + (dev ^ 1), node * devs + dev))
                beside.append((node * devs + dev, (node ^ 1) * devs + dev))
    crossed = [lax.ppermute(w, ALL, across) for w in weights]
    twin = [lax.ppermute(w, ALL, beside) for w in weights]
    twin_crossed = [lax.ppermute(w, ALL, beside) for w in crossed]
    return list(weights) + crossed + twin + twin_crossed


def combine_kernel(shares, returned, out):
    out[...] = dot(shares[...], returned[...]).astype(BF16)


def combine(shares, returned):
    tokens, slots = shares.shape
    width = returned.shape[1]
    tile = 512
    return pl.pallas_call(
        combine_kernel,
        grid=(width // tile,),
        out_shape=jax.ShapeDtypeStruct((tokens, width), BF16),
        in_specs=[
            pl.BlockSpec((tokens, slots), lambda i: (0, 0)),
            pl.BlockSpec((slots, tile), lambda i: (0, i)),
        ],
        out_specs=pl.BlockSpec((tokens, tile), lambda i: (0, i)),
        compiler_params=pltpu.CompilerParams(vmem_limit_bytes=VMEM_BYTES),
        name="combine",
    )(shares, returned)


def listed_prefix(pool_latent, pool_rope, block_table, devices):
    held, block, rank = pool_latent.shape
    rope = pool_rope.shape[2]
    count = block_table.shape[0]
    me = lax.axis_index(ALL)
    mine = block_table // held == me
    slot = block_table % held
    lat = jnp.where(mine[:, None, None], pool_latent[slot], 0).astype(BF16)
    rot = jnp.where(mine[:, None, None], pool_rope[slot], 0).astype(BF16)
    lat = lat.reshape(count * block, rank)
    rot = jnp.transpose(rot, (2, 0, 1)).reshape(rope * count * block // rank, rank)
    both = jnp.concatenate([lat, rot], 0)
    parts = both.reshape(devices, -1, 128)
    arrived = swap(parts, ALL)
    piece = jnp.sum(arrived.astype(F32), axis=0).astype(BF16)
    return swap(jnp.broadcast_to(piece[None], parts.shape), ALL).reshape(both.shape)


def on_device(
    q_nope,
    q_rope,
    kv_latent,
    k_rope,
    pool_latent,
    pool_rope,
    block_table,
    absorb_k,
    absorb_v,
    out_proj,
    residual,
    norm_gain,
    router,
    expert_ids,
    expert_gate,
    expert_up,
    expert_down,
):
    node_count = lax.axis_size("node")
    dev_count = lax.axis_size("dev")
    devices = node_count * dev_count
    tokens, width = residual.shape
    expert_count = router.shape[1]
    cap = max(2, 2 * tokens * expert_ids.shape[1] // expert_count)

    sources = placed_weights((expert_gate, expert_up, expert_down), node_count, dev_count)
    keys_here = jnp.concatenate([kv_latent, k_rope.T], 0)
    keys = lax.all_gather(keys_here, "node", axis=0, tiled=True)
    prefix = listed_prefix(pool_latent, pool_rope, block_table, devices)

    terms = attention(q_nope, q_rope, keys, prefix, absorb_k, absorb_v, out_proj)
    terms = swap(terms.reshape(dev_count, tokens, width), "dev")
    attended, outgoing, shares = route(
        terms, residual, norm_gain.reshape(1, width), router, expert_ids, node_count, cap
    )
    half = cap // 2
    arrived = swap(outgoing.reshape(devices, half, width), ALL)
    served = experts(arrived.reshape(devices * half, width), sources)
    returned = swap(served.reshape(devices, half, width), ALL)
    return attended, combine(shares, returned.reshape(devices * half, width))


def solution(mesh):
    placed = (
        P("node", "dev"),
        P("node", "dev"),
        P("node", None),
        P("node", None),
        P(ALL, None, None),
        P(ALL, None, None),
        P(),
        P("dev", None, None),
        P("dev", None, None),
        P("dev", None),
        P(ALL, None),
        P(),
        P(),
        P(ALL, None),
        P(ALL, None, None),
        P(ALL, None, None),
        P(ALL, None, None),
    )
    return jax.shard_map(
        on_device,
        mesh=mesh,
        in_specs=placed,
        out_specs=(P(ALL, None), P(ALL, None)),
        check_vma=False,
    )
```

```python
import functools
import math

import jax
import jax.numpy as jnp
from jax import lax
from jax.experimental import pallas as pl
from jax.experimental.pallas import tpu as pltpu
from jax.sharding import PartitionSpec as P

ROUTE_SCALE = 2.827
NORM_EPS = 1e-06
FAR_BELOW = -1e30
ALL = ("node", "dev")
VMEM_BYTES = 60 * 1024 * 1024
F32 = jnp.float32
BF16 = jnp.bfloat16


def dot(a, b, dims=(((1,), (0,)), ((), ()))):
    return lax.dot_general(a, b, dims, preferred_element_type=F32)


def swap(value, axis):
    return lax.all_to_all(value, axis, split_axis=0, concat_axis=0, tiled=True)


def fold(q_lat, q_rope, lat, rot, mask, old, new, scale):
    top, total, mixed = new
    heads, tokens = len(q_lat), q_rope.shape[0]
    rope = q_rope.shape[1] // heads
    for h in range(heads):
        rows = pl.ds(h * tokens, tokens)
        scores = dot(q_lat[h], lat, (((1,), (1,)), ((), ())))
        across = (((1,), (0,)), ((), ())) if rot.shape[0] == rope else (((1,), (1,)), ((), ()))
        scores = scores + dot(q_rope[:, h * rope : (h + 1) * rope], rot, across)
        if mask is not None:
            scores = jnp.where(mask, scores, FAR_BELOW)
        row_top = jnp.max(scores, axis=1, keepdims=True)
        if old is not None:
            old_top = old[0][rows]
            row_top = jnp.maximum(row_top, old_top)
        exp_scores = jnp.exp((scores - row_top) * scale)
        row_sum = jnp.sum(exp_scores, axis=1, keepdims=True)
        mix = dot(exp_scores.astype(BF16), lat)
        if old is not None:
            shrink = jnp.exp((old_top - row_top) * scale)
            row_sum = row_sum + old[1][rows] * shrink
            mix = mix + old[2][rows] * shrink
        top[rows] = row_top
        total[rows] = row_sum
        mixed[rows] = mix


def span_kernel(q_nope, q_rope, keys, absorb_k, q_lat, top, total, mixed, *, block):
    heads, nope, rank = absorb_k.shape
    tokens = q_nope.shape[0]
    rope = q_rope.shape[1] // heads
    span = block - rope
    scale = 1.0 / math.sqrt(nope + rope)
    node = lax.axis_index("node")
    first = pl.program_id(0) * tokens
    for h in range(heads):
        part = dot(q_nope[:, h * nope : (h + 1) * nope], absorb_k[h])
        q_lat[h * tokens : (h + 1) * tokens] = part.astype(BF16)

    def add(at, mask, old):
        q_parts = [q_lat[pl.ds(h * tokens, tokens)] for h in range(heads)]
        lat, rot = keys[pl.ds(at, span)], keys[pl.ds(at + span, rope)]
        fold(q_parts, q_rope, lat, rot, mask, old, (top, total, mixed), scale)

    q_pos = first + lax.broadcasted_iota(jnp.int32, (tokens, span), 0)
    key_pos = lax.broadcasted_iota(jnp.int32, (tokens, span), 1)
    add(pl.multiple_of(node * block, 64), key_pos <= q_pos, None)

    def earlier(j, carry):
        add(pl.multiple_of(j * block, 64), None, (top, total, mixed))
        return carry

    lax.fori_loop(0, node, earlier, 0)


def prefix_kernel(
    q_lat,
    q_rope,
    prefix,
    old_top,
    old_total,
    old_mixed,
    absorb_v,
    out_proj,
    terms,
    top,
    total,
    mixed,
    lat,
    *,
    scale,
):
    heads = absorb_v.shape[0]
    tokens = q_rope.shape[0]
    rope = q_rope.shape[1] // heads
    keys, rank = lat.shape
    for c in range(rank // 128):
        lat[:, c * 128 : (c + 1) * 128] = prefix[c * keys : (c + 1) * keys]
    rot = prefix[rank // 128 * keys : (rank // 128 + 1) * keys, :rope]
    q_parts = [q_lat[h * tokens : (h + 1) * tokens] for h in range(heads)]
    old = (old_top, old_total, old_mixed)
    fold(q_parts, q_rope, lat[...], rot, None, old, (top, total, mixed), scale)
    outs = []
    for h in range(heads):
        rows = pl.ds(h * tokens, tokens)
        head_lat = (mixed[rows] / total[rows]).astype(BF16)
        outs.append(dot(head_lat, absorb_v[h]).astype(BF16))
    head_out = jnp.concatenate(outs, axis=1)
    width = out_proj.shape[1]
    step = 512
    for c in range(0, width, step):
        terms[:, c : c + step] = dot(head_out, out_proj[:, c : c + step]).astype(BF16)


def attend_span(q_nope, q_rope, keys, absorb_k, block):
    rows = q_nope.shape[0]
    tile = min(256, rows)
    heads, nope, rank = absorb_k.shape
    whole = pl.BlockSpec(memory_space=pltpu.VMEM)
    state = [
        jax.ShapeDtypeStruct((heads * rows, rank), BF16),
        jax.ShapeDtypeStruct((heads * rows, 1), F32),
        jax.ShapeDtypeStruct((heads * rows, 1), F32),
        jax.ShapeDtypeStruct((heads * rows, rank), F32),
    ]
    pairs = heads * rows * keys.shape[0]
    return pl.pallas_call(
        functools.partial(span_kernel, block=block),
        grid=(rows // tile,),
        out_shape=state,
        in_specs=[
            pl.BlockSpec((tile, q_nope.shape[1]), lambda i: (i, 0)),
            pl.BlockSpec((tile, q_rope.shape[1]), lambda i: (i, 0)),
            whole,
            whole,
        ],
        out_specs=[pl.BlockSpec((heads * tile, s.shape[1]), lambda i: (i, 0)) for s in state],
        compiler_params=pltpu.CompilerParams(vmem_limit_bytes=VMEM_BYTES),
        cost_estimate=pl.CostEstimate(
            flops=2 * pairs * (2 * rank + 64), bytes_accessed=8 << 20, transcendentals=pairs
        ),
        name="attend_span",
    )(q_nope, q_rope, keys, absorb_k)


def attend_prefix(state, q_rope, prefix, absorb_v, out_proj, nope, keys):
    rows = q_rope.shape[0]
    tile = min(256, rows)
    heads, rank, _ = absorb_v.shape
    rope = q_rope.shape[1] // heads
    width = out_proj.shape[1]
    whole = pl.BlockSpec(memory_space=pltpu.VMEM)
    specs = [pl.BlockSpec((heads * tile, s.shape[1]), lambda i: (i, 0)) for s in state]
    return pl.pallas_call(
        functools.partial(prefix_kernel, scale=1.0 / math.sqrt(nope + rope)),
        grid=(rows // tile,),
        out_shape=jax.ShapeDtypeStruct((rows, width), BF16),
        in_specs=[
            specs[0],
            pl.BlockSpec((tile, q_rope.shape[1]), lambda i: (i, 0)),
            whole,
            specs[1],
            specs[2],
            specs[3],
            whole,
            whole,
        ],
        out_specs=pl.BlockSpec((tile, width), lambda i: (i, 0)),
        scratch_shapes=[
            pltpu.VMEM((heads * tile, 1), F32),
            pltpu.VMEM((heads * tile, 1), F32),
            pltpu.VMEM((heads * tile, rank), F32),
            pltpu.VMEM((keys, rank), BF16),
        ],
        compiler_params=pltpu.CompilerParams(vmem_limit_bytes=VMEM_BYTES),
        cost_estimate=pl.CostEstimate(flops=6 << 30, bytes_accessed=10 << 20, transcendentals=0),
        name="attend_prefix",
    )(state[0], q_rope, prefix, state[1], state[2], state[3], absorb_v, out_proj)


def slot_place(column, nodes, cap, experts):
    half = cap // 2
    devs = 2 * experts // nodes
    device, part, low = column // cap, column % cap // half, column % half
    node, dev = device // devs, device % devs
    expert = (experts // nodes) * (node // 2 * 2 + dev % 2) + dev // 2
    return expert, node % 2 * half + low, part


def route_kernel(terms, residual, gain, router, ids, attended, outgoing, shares, *, nodes, cap):
    groups, tokens, width = terms.shape
    experts = router.shape[1]
    top_k = ids.shape[1]
    acc = terms[0].astype(F32)
    for g in range(1, groups):
        acc = acc + terms[g].astype(F32)
    stream = (residual[...].astype(F32) + acc).astype(BF16)
    attended[...] = stream
    stream = stream.astype(F32)
    mean = jnp.mean(stream * stream, axis=1, keepdims=True)
    normed = (stream * lax.rsqrt(mean + NORM_EPS) * gain[...].astype(F32)).astype(BF16)
    logits = dot(normed, router[...])
    expert = lax.broadcasted_iota(jnp.int32, (tokens, experts), 1)
    hits = [ids[:, j : j + 1] == expert for j in range(top_k)]
    gates = [
        jax.nn.sigmoid(jnp.sum(jnp.where(hit, logits, 0.0), axis=1, keepdims=True)) for hit in hits
    ]
    gate_sum = functools.reduce(lambda a, b: a + b, gates)
    weight = jnp.zeros((tokens, experts), F32)
    used = jnp.zeros((tokens, experts), F32)
    for hit, gate in zip(hits, gates):
        weight = jnp.where(hit, ROUTE_SCALE * gate / gate_sum, weight)
        used = jnp.where(hit, 1.0, used)
    weight = weight.astype(BF16)
    used = used.astype(BF16)
    below = lax.broadcasted_iota(jnp.int32, (tokens, tokens), 1) < lax.broadcasted_iota(
        jnp.int32, (tokens, tokens), 0
    )
    rank = dot(below.astype(BF16), used).astype(BF16)
    rows = 2 * experts * cap
    owner = slot_place(lax.broadcasted_iota(jnp.int32, (experts, rows), 1), nodes, cap, experts)[0]
    spread = (owner == lax.broadcasted_iota(jnp.int32, (experts, rows), 0)).astype(BF16)
    _, slot, part = slot_place(
        lax.broadcasted_iota(jnp.int32, (tokens, rows), 1), nodes, cap, experts
    )
    filled = (dot(used, spread) > 0.5) & (dot(rank, spread) == slot.astype(F32))
    share = jnp.where(filled, dot(weight, spread), 0.0)
    filled = filled.astype(F32)
    share = [jnp.where(part == p, share, 0.0) for p in range(2)]
    filled = [jnp.where(part == p, filled, 0.0) for p in range(2)]
    shares[...] = jnp.concatenate(share, 0).astype(BF16)
    fill = jnp.concatenate(filled, 0).astype(BF16)
    narrow = width // 2
    halves = jnp.concatenate([normed[:, :narrow], normed[:, narrow:]], 0)
    step = narrow // 2
    for c in range(0, narrow, step):
        outgoing[:, c : c + step] = dot(
            fill, halves[:, c : c + step], (((0,), (0,)), ((), ()))
        ).astype(BF16)


def route(terms, residual, gain, router, ids, nodes, cap):
    tokens, width = residual.shape
    rows = 2 * router.shape[1] * cap
    whole = pl.BlockSpec(memory_space=pltpu.VMEM)
    return pl.pallas_call(
        functools.partial(route_kernel, nodes=nodes, cap=cap),
        out_shape=(
            jax.ShapeDtypeStruct((tokens, width), BF16),
            jax.ShapeDtypeStruct((rows, width // 2), BF16),
            jax.ShapeDtypeStruct((2 * tokens, rows), BF16),
        ),
        in_specs=[whole] * 5,
        out_specs=(whole, whole, whole),
        compiler_params=pltpu.CompilerParams(vmem_limit_bytes=VMEM_BYTES),
        name="route",
    )(terms, residual, gain, router, ids)


def expert_kernel(rows, *refs, cap):
    sources, (out, whole_rows, gates, ups, downs, sems) = refs[:12], refs[12:]
    node, dev = lax.axis_index("node"), lax.axis_index("dev")
    keeper = node % 2 == dev % 2
    own, crossed, twin, twin_crossed = (sources[3 * i : 3 * i + 3] for i in range(4))
    slots = (gates, ups, downs)

    def copy(source, share, part):
        return pltpu.make_async_copy(
            source[part].at[0], slots[part].at[share], sems.at[share * 3 + part]
        )

    order = ((0, 0), (0, 1), (1, 0), (1, 1), (0, 2), (1, 2))

    @pl.when(keeper)
    def _():
        for share, part in order:
            copy((own, crossed)[share], share, part).start()

    @pl.when(jnp.logical_not(keeper))
    def _():
        for share, part in order:
            copy((twin, twin_crossed)[share], share, part).start()

    count, narrow = rows.shape
    block = 256
    half = cap // 2
    here = lax.broadcasted_iota(jnp.int32, (block, block), 0)
    there = lax.broadcasted_iota(jnp.int32, (block, block), 1)
    mid = block // 2
    wanted = here % mid // half * cap + here // mid * half + here % half
    order_rows = (there == wanted).astype(F32).astype(BF16)
    for b in range(0, count, block):
        sorted_rows = dot(order_rows, rows[b : b + block]).astype(BF16)
        whole_rows[b // 2 : b // 2 + mid, :narrow] = sorted_rows[:mid]
        whole_rows[b // 2 : b // 2 + mid, narrow:] = sorted_rows[mid:]

    x = whole_rows[...]
    hidden = []
    for share in range(2):
        copy(own, share, 0).wait()
        gate_act = dot(x, gates[share])
        copy(own, share, 1).wait()
        up_act = dot(x, ups[share])
        hidden.append((jax.nn.silu(gate_act) * up_act).astype(BF16))
    for share in range(2):
        copy(own, share, 2).wait()
    step = narrow // 2
    for c in range(0, narrow, step):
        parts = []
        for at in (c, narrow + c):
            part = dot(hidden[0], downs[0, :, at : at + step])
            part = part + dot(hidden[1], downs[1, :, at : at + step])
            parts.append(part.astype(BF16))
        for b in range(0, count, block):
            both = jnp.concatenate([part[b // 2 : b // 2 + mid] for part in parts], 0)
            out[b : b + block, c : c + step] = dot(
                order_rows, both, (((0,), (0,)), ((), ()))
            ).astype(BF16)


def experts(rows, sources, cap):
    count, narrow = rows.shape
    _, width, hidden = sources[0].shape
    whole = pl.BlockSpec(memory_space=pltpu.VMEM)
    return pl.pallas_call(
        functools.partial(expert_kernel, cap=cap),
        out_shape=jax.ShapeDtypeStruct((count, narrow), BF16),
        in_specs=[whole] + [pl.BlockSpec(memory_space=pl.ANY)] * 12,
        out_specs=whole,
        scratch_shapes=[
            pltpu.VMEM((count // 2, width), BF16),
            pltpu.VMEM((2, width, hidden), BF16),
            pltpu.VMEM((2, width, hidden), BF16),
            pltpu.VMEM((2, hidden, width), BF16),
            pltpu.SemaphoreType.DMA((6,)),
        ],
        compiler_params=pltpu.CompilerParams(vmem_limit_bytes=VMEM_BYTES),
        name="experts",
    )(rows, *sources)


def placed_weights(weights, nodes, devs):
    across, beside = [], []
    for node in range(nodes):
        for dev in range(devs):
            if node % 2 == dev % 2:
                across.append((node * devs + (dev ^ 1), node * devs + dev))
                beside.append((node * devs + dev, (node ^ 1) * devs + dev))
    crossed = [lax.ppermute(w, ALL, across) for w in weights]

    def place_last(crossed, last):
        own = list(weights) + [last]
        crossed = list(crossed) + [lax.ppermute(last, ALL, across)]
        twin = [lax.ppermute(w, ALL, beside) for w in own]

        def finish(crossed):
            twin_crossed = [lax.ppermute(w, ALL, beside) for w in crossed]
            return own + list(crossed) + twin + twin_crossed

        return crossed, finish

    return crossed, place_last


def combine_kernel(shares, returned, out):
    tokens, width = out.shape
    tile = returned.shape[1]
    both = dot(shares[...], returned[...]).astype(BF16)
    at = pl.multiple_of(pl.program_id(0) * tile, 128)
    out[:, pl.ds(at, tile)] = both[:tokens]
    at = pl.multiple_of(width // 2 + pl.program_id(0) * tile, 128)
    out[:, pl.ds(at, tile)] = both[tokens:]


def combine(shares, returned):
    tokens, rows = shares.shape[0] // 2, shares.shape[1]
    narrow = returned.shape[1]
    tile = 256
    return pl.pallas_call(
        combine_kernel,
        grid=(narrow // tile,),
        out_shape=jax.ShapeDtypeStruct((tokens, 2 * narrow), BF16),
        in_specs=[
            pl.BlockSpec((2 * tokens, rows), lambda i: (0, 0)),
            pl.BlockSpec((rows, tile), lambda i: (0, i)),
        ],
        out_specs=pl.BlockSpec((tokens, 2 * narrow), lambda i: (0, 0)),
        compiler_params=pltpu.CompilerParams(vmem_limit_bytes=VMEM_BYTES),
        name="combine",
    )(shares, returned)


def listed_kernel(table, lat, rot, out):
    held, block, rank = lat.shape
    rope = rot.shape[2]
    count = table.shape[0]
    me = lax.axis_index("node") * lax.axis_size("dev") + lax.axis_index("dev")
    out[...] = jnp.zeros(out.shape, BF16)
    for b in range(count):
        entry = table[b]
        slot = entry % held

        @pl.when(entry // held == me)
        def _():
            for c in range(rank // 128):
                at = (c * count + b) * block
                out[at : at + block] = lat[slot, :, c * 128 : (c + 1) * 128]
            at = (rank // 128 * count + b) * block
            out[at : at + block, :rope] = rot[slot]


def spread_kernel(arrived, *refs):
    out = refs[-1]
    count = arrived.shape[0]
    piece = arrived[0].astype(F32)
    for d in range(1, count):
        piece = piece + arrived[d].astype(F32)
    out[...] = jnp.broadcast_to(piece.astype(BF16)[None], out.shape)


def listed_prefix(pool_latent, pool_rope, block_table, devices, first):
    held, block, rank = pool_latent.shape
    keys = block_table.shape[0] * block
    rows = -(-keys * (rank // 128 + 1) // (devices * 8)) * devices * 8
    whole = pl.BlockSpec(memory_space=pltpu.VMEM)
    mine = pl.pallas_call(
        listed_kernel,
        out_shape=jax.ShapeDtypeStruct((rows, 128), BF16),
        in_specs=[pl.BlockSpec(memory_space=pltpu.SMEM), whole, whole],
        out_specs=whole,
        compiler_params=pltpu.CompilerParams(vmem_limit_bytes=VMEM_BYTES),
        name="listed",
    )(block_table, pool_latent, pool_rope)
    arrived = swap(mine.reshape(devices, rows // devices, 128), ALL)
    state, crossed, last = first
    spread = pl.pallas_call(
        spread_kernel,
        out_shape=jax.ShapeDtypeStruct(arrived.shape, BF16),
        in_specs=[whole] + [pl.BlockSpec(memory_space=pl.ANY)] * len(state),
        out_specs=whole,
        compiler_params=pltpu.CompilerParams(vmem_limit_bytes=VMEM_BYTES),
        name="spread",
    )(arrived, *state)
    spread, crossed, last = lax.optimization_barrier((spread, crossed, last))
    return swap(spread, ALL).reshape(rows, 128), (state, crossed, last)


def on_device(
    q_nope,
    q_rope,
    kv_latent,
    k_rope,
    pool_latent,
    pool_rope,
    block_table,
    absorb_k,
    absorb_v,
    out_proj,
    residual,
    norm_gain,
    router,
    expert_ids,
    expert_gate,
    expert_up,
    expert_down,
):
    node_count = lax.axis_size("node")
    dev_count = lax.axis_size("dev")
    devices = node_count * dev_count
    prefix_keys = block_table.shape[0] * pool_latent.shape[1]
    tokens, width = residual.shape
    expert_count = router.shape[1]
    cap = max(2, 2 * tokens * expert_ids.shape[1] // expert_count)

    crossed, place_last = placed_weights((expert_gate, expert_up), node_count, dev_count)
    keys_here = jnp.concatenate([kv_latent, k_rope.T], 0)
    keys = lax.all_gather(keys_here, "node", axis=0, tiled=True)
    state = attend_span(q_nope, q_rope, keys, absorb_k, keys_here.shape[0])
    prefix, (state, crossed, expert_down) = listed_prefix(
        pool_latent, pool_rope, block_table, devices, (state, crossed, expert_down)
    )
    crossed, finish = place_last(crossed, expert_down)
    terms = attend_prefix(
        state, q_rope, prefix, absorb_v, out_proj, absorb_k.shape[1], prefix_keys
    )
    terms, crossed[1] = lax.optimization_barrier((terms, crossed[1]))
    terms = swap(terms.reshape(dev_count, tokens, width), "dev")
    terms, crossed[2] = lax.optimization_barrier((terms, crossed[2]))
    attended, outgoing, shares = route(
        terms, residual, norm_gain.reshape(1, width), router, expert_ids, node_count, cap
    )
    arrived = swap(outgoing.reshape(devices, cap, width // 2), ALL)
    served = experts(arrived.reshape(devices * cap, width // 2), finish(crossed), cap)
    returned = swap(served.reshape(devices, cap, width // 2), ALL)
    return attended, combine(shares, returned.reshape(devices * cap, width // 2))


def solution(mesh):
    placed = (
        P("node", "dev"),
        P("node", "dev"),
        P("node", None),
        P("node", None),
        P(ALL, None, None),
        P(ALL, None, None),
        P(),
        P("dev", None, None),
        P("dev", None, None),
        P("dev", None),
        P(ALL, None),
        P(),
        P(),
        P(ALL, None),
        P(ALL, None, None),
        P(ALL, None, None),
        P(ALL, None, None),
    )
    return jax.shard_map(
        on_device,
        mesh=mesh,
        in_specs=placed,
        out_specs=(P(ALL, None), P(ALL, None)),
        check_vma=False,
    )
```

```python
import functools
import math

import jax
import jax.numpy as jnp
from jax import lax
from jax.experimental import pallas as pl
from jax.experimental.pallas import tpu as pltpu
from jax.sharding import PartitionSpec as P

ROUTE_SCALE = 2.827
NORM_EPS = 1e-06
FAR_BELOW = -1e30
ALL = ("node", "dev")
VMEM_BYTES = 60 * 1024 * 1024
F32 = jnp.float32
BF16 = jnp.bfloat16


def dot(a, b, dims=(((1,), (0,)), ((), ()))):
    return lax.dot_general(a, b, dims, preferred_element_type=F32)


def swap(value, axis):
    return lax.all_to_all(value, axis, split_axis=0, concat_axis=0, tiled=True)


def fold(q_lat, q_rope, lat, rot, mask, old, new, scale):
    top, total, mixed = new
    heads, tokens = len(q_lat), q_rope.shape[0]
    rope = q_rope.shape[1] // heads
    for h in range(heads):
        rows = pl.ds(h * tokens, tokens)
        scores = dot(q_lat[h], lat, (((1,), (1,)), ((), ())))
        across = (((1,), (0,)), ((), ())) if rot.shape[0] == rope else (((1,), (1,)), ((), ()))
        scores = scores + dot(q_rope[:, h * rope : (h + 1) * rope], rot, across)
        if mask is not None:
            scores = jnp.where(mask, scores, FAR_BELOW)
        row_top = jnp.max(scores, axis=1, keepdims=True)
        if old is not None:
            old_top = old[0][rows]
            row_top = jnp.maximum(row_top, old_top)
        exp_scores = jnp.exp((scores - row_top) * scale)
        row_sum = jnp.sum(exp_scores, axis=1, keepdims=True)
        mix = dot(exp_scores.astype(BF16), lat)
        if old is not None:
            shrink = jnp.exp((old_top - row_top) * scale)
            row_sum = row_sum + old[1][rows] * shrink
            mix = mix + old[2][rows] * shrink
        top[rows] = row_top
        total[rows] = row_sum
        mixed[rows] = mix


def span_kernel(q_nope, q_rope, keys, absorb_k, q_lat, top, total, mixed, *, block):
    heads, nope, rank = absorb_k.shape
    tokens = q_nope.shape[0]
    rope = q_rope.shape[1] // heads
    span = block - rope
    scale = 1.0 / math.sqrt(nope + rope)
    node = lax.axis_index("node")
    first = pl.program_id(0) * tokens
    for h in range(heads):
        part = dot(q_nope[:, h * nope : (h + 1) * nope], absorb_k[h])
        q_lat[h * tokens : (h + 1) * tokens] = part.astype(BF16)

    def add(at, mask, old):
        q_parts = [q_lat[pl.ds(h * tokens, tokens)] for h in range(heads)]
        lat, rot = keys[pl.ds(at, span)], keys[pl.ds(at + span, rope)]
        fold(q_parts, q_rope, lat, rot, mask, old, (top, total, mixed), scale)

    q_pos = first + lax.broadcasted_iota(jnp.int32, (tokens, span), 0)
    key_pos = lax.broadcasted_iota(jnp.int32, (tokens, span), 1)
    add(pl.multiple_of(node * block, 64), key_pos <= q_pos, None)

    def earlier(j, carry):
        add(pl.multiple_of(j * block, 64), None, (top, total, mixed))
        return carry

    lax.fori_loop(0, node, earlier, 0)


def prefix_kernel(
    q_lat,
    q_rope,
    prefix,
    old_top,
    old_total,
    old_mixed,
    absorb_v,
    out_proj,
    terms,
    top,
    total,
    mixed,
    lat,
    *,
    scale,
):
    heads = absorb_v.shape[0]
    tokens = q_rope.shape[0]
    rope = q_rope.shape[1] // heads
    keys, rank = lat.shape
    for c in range(rank // 128):
        lat[:, c * 128 : (c + 1) * 128] = prefix[c * keys : (c + 1) * keys]
    rot = prefix[rank // 128 * keys : (rank // 128 + 1) * keys, :rope]
    q_parts = [q_lat[h * tokens : (h + 1) * tokens] for h in range(heads)]
    old = (old_top, old_total, old_mixed)
    fold(q_parts, q_rope, lat[...], rot, None, old, (top, total, mixed), scale)
    outs = []
    for h in range(heads):
        rows = pl.ds(h * tokens, tokens)
        head_lat = (mixed[rows] / total[rows]).astype(BF16)
        outs.append(dot(head_lat, absorb_v[h]).astype(BF16))
    head_out = jnp.concatenate(outs, axis=1)
    width = out_proj.shape[1]
    step = 512
    for c in range(0, width, step):
        terms[:, c : c + step] = dot(head_out, out_proj[:, c : c + step]).astype(BF16)


def attend_span(q_nope, q_rope, keys, absorb_k, block):
    rows = q_nope.shape[0]
    tile = min(256, rows)
    heads, nope, rank = absorb_k.shape
    whole = pl.BlockSpec(memory_space=pltpu.VMEM)
    state = [
        jax.ShapeDtypeStruct((heads * rows, rank), BF16),
        jax.ShapeDtypeStruct((heads * rows, 1), F32),
        jax.ShapeDtypeStruct((heads * rows, 1), F32),
        jax.ShapeDtypeStruct((heads * rows, rank), F32),
    ]
    pairs = heads * rows * keys.shape[0]
    return pl.pallas_call(
        functools.partial(span_kernel, block=block),
        grid=(rows // tile,),
        out_shape=state,
        in_specs=[
            pl.BlockSpec((tile, q_nope.shape[1]), lambda i: (i, 0)),
            pl.BlockSpec((tile, q_rope.shape[1]), lambda i: (i, 0)),
            whole,
            whole,
        ],
        out_specs=[pl.BlockSpec((heads * tile, s.shape[1]), lambda i: (i, 0)) for s in state],
        compiler_params=pltpu.CompilerParams(vmem_limit_bytes=VMEM_BYTES),
        cost_estimate=pl.CostEstimate(
            flops=2 * pairs * (2 * rank + 64), bytes_accessed=8 << 20, transcendentals=pairs
        ),
        name="attend_span",
    )(q_nope, q_rope, keys, absorb_k)


def attend_prefix(state, q_rope, prefix, absorb_v, out_proj, nope, keys):
    rows = q_rope.shape[0]
    tile = min(256, rows)
    heads, rank, _ = absorb_v.shape
    rope = q_rope.shape[1] // heads
    width = out_proj.shape[1]
    whole = pl.BlockSpec(memory_space=pltpu.VMEM)
    specs = [pl.BlockSpec((heads * tile, s.shape[1]), lambda i: (i, 0)) for s in state]
    return pl.pallas_call(
        functools.partial(prefix_kernel, scale=1.0 / math.sqrt(nope + rope)),
        grid=(rows // tile,),
        out_shape=jax.ShapeDtypeStruct((rows, width), BF16),
        in_specs=[
            specs[0],
            pl.BlockSpec((tile, q_rope.shape[1]), lambda i: (i, 0)),
            whole,
            specs[1],
            specs[2],
            specs[3],
            whole,
            whole,
        ],
        out_specs=pl.BlockSpec((tile, width), lambda i: (i, 0)),
        scratch_shapes=[
            pltpu.VMEM((heads * tile, 1), F32),
            pltpu.VMEM((heads * tile, 1), F32),
            pltpu.VMEM((heads * tile, rank), F32),
            pltpu.VMEM((keys, rank), BF16),
        ],
        compiler_params=pltpu.CompilerParams(vmem_limit_bytes=VMEM_BYTES),
        cost_estimate=pl.CostEstimate(flops=6 << 30, bytes_accessed=10 << 20, transcendentals=0),
        name="attend_prefix",
    )(state[0], q_rope, prefix, state[1], state[2], state[3], absorb_v, out_proj)


def slot_place(column, nodes, cap, experts):
    half = cap // 2
    devs = 2 * experts // nodes
    device, part, low = column // cap, column % cap // half, column % half
    node, dev = device // devs, device % devs
    expert = (experts // nodes) * (node // 2 * 2 + dev % 2) + dev // 2
    return expert, node % 2 * half + low, part


def route_kernel(terms, residual, gain, router, ids, attended, outgoing, shares, *, nodes, cap):
    groups, tokens, width = terms.shape
    experts = router.shape[0]
    top_k = ids.shape[1]
    acc = terms[0].astype(F32)
    for g in range(1, groups):
        acc = acc + terms[g].astype(F32)
    stream = (residual[...].astype(F32) + acc).astype(BF16)
    attended[...] = stream
    stream = stream.astype(F32)
    mean = jnp.mean(stream * stream, axis=1, keepdims=True)
    normed = (stream * lax.rsqrt(mean + NORM_EPS) * gain[...].astype(F32)).astype(BF16)
    logits = dot(normed, router[...], (((1,), (1,)), ((), ())))
    expert = lax.broadcasted_iota(jnp.int32, (tokens, experts), 1)
    hits = [ids[:, j : j + 1] == expert for j in range(top_k)]
    gates = [
        jax.nn.sigmoid(jnp.sum(jnp.where(hit, logits, 0.0), axis=1, keepdims=True)) for hit in hits
    ]
    gate_sum = functools.reduce(lambda a, b: a + b, gates)
    weight = jnp.zeros((tokens, experts), F32)
    used = jnp.zeros((tokens, experts), F32)
    for hit, gate in zip(hits, gates):
        weight = jnp.where(hit, ROUTE_SCALE * gate / gate_sum, weight)
        used = jnp.where(hit, 1.0, used)
    weight = weight.astype(BF16)
    used = used.astype(BF16)
    below = lax.broadcasted_iota(jnp.int32, (tokens, tokens), 1) < lax.broadcasted_iota(
        jnp.int32, (tokens, tokens), 0
    )
    rank = dot(below.astype(BF16), used).astype(BF16)
    rows = 2 * experts * cap
    owner = slot_place(lax.broadcasted_iota(jnp.int32, (experts, rows), 1), nodes, cap, experts)[0]
    spread = (owner == lax.broadcasted_iota(jnp.int32, (experts, rows), 0)).astype(BF16)
    _, slot, part = slot_place(
        lax.broadcasted_iota(jnp.int32, (tokens, rows), 1), nodes, cap, experts
    )
    filled = (dot(used, spread) > 0.5) & (dot(rank, spread) == slot.astype(F32))
    share = jnp.where(filled, dot(weight, spread), 0.0)
    filled = filled.astype(F32)
    share = [jnp.where(part == p, share, 0.0) for p in range(2)]
    filled = [jnp.where(part == p, filled, 0.0) for p in range(2)]
    shares[...] = jnp.concatenate(share, 0).astype(BF16)
    fill = jnp.concatenate(filled, 0).astype(BF16)
    narrow = width // 2
    halves = jnp.concatenate([normed[:, :narrow], normed[:, narrow:]], 0)
    step = narrow // 2
    for c in range(0, narrow, step):
        outgoing[:, c : c + step] = dot(
            fill, halves[:, c : c + step], (((0,), (0,)), ((), ()))
        ).astype(BF16)


def route(terms, residual, gain, router, ids, nodes, cap):
    tokens, width = residual.shape
    rows = 2 * router.shape[0] * cap
    whole = pl.BlockSpec(memory_space=pltpu.VMEM)
    return pl.pallas_call(
        functools.partial(route_kernel, nodes=nodes, cap=cap),
        out_shape=(
            jax.ShapeDtypeStruct((tokens, width), BF16),
            jax.ShapeDtypeStruct((rows, width // 2), BF16),
            jax.ShapeDtypeStruct((2 * tokens, rows), BF16),
        ),
        in_specs=[whole] * 5,
        out_specs=(whole, whole, whole),
        compiler_params=pltpu.CompilerParams(vmem_limit_bytes=VMEM_BYTES),
        name="route",
    )(terms, residual, gain, router, ids)


def expert_kernel(rows, *refs, cap):
    sources, (out, whole_rows, gates, ups, downs, sems) = refs[:12], refs[12:]
    node, dev = lax.axis_index("node"), lax.axis_index("dev")
    keeper = node % 2 == dev % 2
    own, crossed, twin, twin_crossed = (sources[3 * i : 3 * i + 3] for i in range(4))
    slots = (gates, ups, downs)

    def copy(source, share, part):
        return pltpu.make_async_copy(
            source[part].at[0], slots[part].at[share], sems.at[share * 3 + part]
        )

    order = ((0, 0), (0, 1), (1, 0), (1, 1), (0, 2), (1, 2))

    @pl.when(keeper)
    def _():
        for share, part in order:
            copy((own, crossed)[share], share, part).start()

    @pl.when(jnp.logical_not(keeper))
    def _():
        for share, part in order:
            copy((twin, twin_crossed)[share], share, part).start()

    count, narrow = rows.shape
    block = 256
    half = cap // 2
    here = lax.broadcasted_iota(jnp.int32, (block, block), 0)
    there = lax.broadcasted_iota(jnp.int32, (block, block), 1)
    mid = block // 2
    wanted = here % mid // half * cap + here // mid * half + here % half
    order_rows = (there == wanted).astype(F32).astype(BF16)
    for b in range(0, count, block):
        sorted_rows = dot(order_rows, rows[b : b + block]).astype(BF16)
        whole_rows[b // 2 : b // 2 + mid, :narrow] = sorted_rows[:mid]
        whole_rows[b // 2 : b // 2 + mid, narrow:] = sorted_rows[mid:]

    x = whole_rows[...]
    hidden = []
    for share in range(2):
        copy(own, share, 0).wait()
        gate_act = dot(x, gates[share])
        copy(own, share, 1).wait()
        up_act = dot(x, ups[share])
        hidden.append((jax.nn.silu(gate_act) * up_act).astype(BF16))
    for share in range(2):
        copy(own, share, 2).wait()
    step = narrow // 2
    for c in range(0, narrow, step):
        parts = []
        for at in (c, narrow + c):
            part = dot(hidden[0], downs[0, :, at : at + step])
            part = part + dot(hidden[1], downs[1, :, at : at + step])
            parts.append(part.astype(BF16))
        for b in range(0, count, block):
            both = jnp.concatenate([part[b // 2 : b // 2 + mid] for part in parts], 0)
            out[b : b + block, c : c + step] = dot(
                order_rows, both, (((0,), (0,)), ((), ()))
            ).astype(BF16)


def experts(rows, sources, cap):
    count, narrow = rows.shape
    _, width, hidden = sources[0].shape
    whole = pl.BlockSpec(memory_space=pltpu.VMEM)
    return pl.pallas_call(
        functools.partial(expert_kernel, cap=cap),
        out_shape=jax.ShapeDtypeStruct((count, narrow), BF16),
        in_specs=[whole] + [pl.BlockSpec(memory_space=pl.ANY)] * 12,
        out_specs=whole,
        scratch_shapes=[
            pltpu.VMEM((count // 2, width), BF16),
            pltpu.VMEM((2, width, hidden), BF16),
            pltpu.VMEM((2, width, hidden), BF16),
            pltpu.VMEM((2, hidden, width), BF16),
            pltpu.SemaphoreType.DMA((6,)),
        ],
        compiler_params=pltpu.CompilerParams(vmem_limit_bytes=VMEM_BYTES),
        name="experts",
    )(rows, *sources)


def placed_weights(weights, nodes, devs):
    across, beside = [], []
    for node in range(nodes):
        for dev in range(devs):
            if node % 2 == dev % 2:
                across.append((node * devs + (dev ^ 1), node * devs + dev))
            beside.append((node * devs + dev, (node ^ 1) * devs + dev))
    crossed = [lax.ppermute(w, ALL, across) for w in weights]

    def place_last(crossed, last):
        own = list(weights) + [last]
        crossed = list(crossed) + [lax.ppermute(last, ALL, across)]
        twin = [lax.ppermute(w, ALL, beside) for w in own]

        def finish(crossed):
            twin_crossed = [lax.ppermute(w, ALL, beside) for w in crossed]
            return own + list(crossed) + twin + twin_crossed

        return crossed, finish

    return crossed, place_last


def combine_kernel(shares, returned, out, total):
    tokens, width = out.shape
    part = dot(shares[...], returned[...])
    step = pl.program_id(0)

    @pl.when(step == 0)
    def _():
        total[...] = part

    @pl.when(step > 0)
    def _():
        total[...] += part

    @pl.when(step == pl.num_programs(0) - 1)
    def _():
        out[:, : width // 2] = total[:tokens].astype(BF16)
        out[:, width // 2 :] = total[tokens:].astype(BF16)


def combine(shares, returned):
    tokens, rows = shares.shape[0] // 2, shares.shape[1]
    narrow = returned.shape[1]
    tile = 256
    return pl.pallas_call(
        combine_kernel,
        grid=(rows // tile,),
        out_shape=jax.ShapeDtypeStruct((tokens, 2 * narrow), BF16),
        in_specs=[
            pl.BlockSpec((2 * tokens, tile), lambda i: (0, i)),
            pl.BlockSpec((tile, narrow), lambda i: (i, 0)),
        ],
        out_specs=pl.BlockSpec((tokens, 2 * narrow), lambda i: (0, 0)),
        scratch_shapes=[pltpu.VMEM((2 * tokens, narrow), F32)],
        compiler_params=pltpu.CompilerParams(vmem_limit_bytes=VMEM_BYTES),
        name="combine",
    )(shares, returned)


def listed_kernel(table, lat, rot, out):
    held, block, rank = lat.shape
    rope = rot.shape[2]
    count = table.shape[0]
    me = lax.axis_index("node") * lax.axis_size("dev") + lax.axis_index("dev")
    out[...] = jnp.zeros(out.shape, BF16)
    for b in range(count):
        entry = table[b]
        slot = entry % held

        @pl.when(entry // held == me)
        def _():
            for c in range(rank // 128):
                at = (c * count + b) * block
                out[at : at + block] = lat[slot, :, c * 128 : (c + 1) * 128]
            at = (rank // 128 * count + b) * block
            out[at : at + block, :rope] = rot[slot]


def spread_kernel(arrived, *refs):
    out = refs[-1]
    count = arrived.shape[0]
    piece = arrived[0].astype(F32)
    for d in range(1, count):
        piece = piece + arrived[d].astype(F32)
    out[...] = jnp.broadcast_to(piece.astype(BF16)[None], out.shape)


def listed_prefix(pool_latent, pool_rope, block_table, devices, first):
    held, block, rank = pool_latent.shape
    keys = block_table.shape[0] * block
    rows = -(-keys * (rank // 128 + 1) // (devices * 8)) * devices * 8
    whole = pl.BlockSpec(memory_space=pltpu.VMEM)
    mine = pl.pallas_call(
        listed_kernel,
        out_shape=jax.ShapeDtypeStruct((rows, 128), BF16),
        in_specs=[pl.BlockSpec(memory_space=pltpu.SMEM), whole, whole],
        out_specs=whole,
        compiler_params=pltpu.CompilerParams(vmem_limit_bytes=VMEM_BYTES),
        name="listed",
    )(block_table, pool_latent, pool_rope)
    arrived = swap(mine.reshape(devices, rows // devices, 128), ALL)
    state, crossed, last = first
    spread = pl.pallas_call(
        spread_kernel,
        out_shape=jax.ShapeDtypeStruct(arrived.shape, BF16),
        in_specs=[whole] + [pl.BlockSpec(memory_space=pl.ANY)] * len(state),
        out_specs=whole,
        compiler_params=pltpu.CompilerParams(vmem_limit_bytes=VMEM_BYTES),
        name="spread",
    )(arrived, *state)
    spread, crossed, last = lax.optimization_barrier((spread, crossed, last))
    return swap(spread, ALL).reshape(rows, 128), (state, crossed, last)


def on_device(
    q_nope,
    q_rope,
    kv_latent,
    k_rope,
    pool_latent,
    pool_rope,
    block_table,
    absorb_k,
    absorb_v,
    out_proj,
    residual,
    norm_gain,
    router,
    expert_ids,
    expert_gate,
    expert_up,
    expert_down,
):
    node_count = lax.axis_size("node")
    dev_count = lax.axis_size("dev")
    devices = node_count * dev_count
    prefix_keys = block_table.shape[0] * pool_latent.shape[1]
    tokens, width = residual.shape
    expert_count = router.shape[1]
    cap = max(2, 2 * tokens * expert_ids.shape[1] // expert_count)

    crossed, place_last = placed_weights((expert_gate, expert_up), node_count, dev_count)
    keys_here = jnp.concatenate([kv_latent, k_rope.T], 0)
    keys = lax.all_gather(keys_here, "node", axis=0, tiled=True)
    state = attend_span(q_nope, q_rope, keys, absorb_k, keys_here.shape[0])
    prefix, (state, crossed, expert_down) = listed_prefix(
        pool_latent, pool_rope, block_table, devices, (state, crossed, expert_down)
    )
    crossed, finish = place_last(crossed, expert_down)
    terms = attend_prefix(
        state, q_rope, prefix, absorb_v, out_proj, absorb_k.shape[1], prefix_keys
    )
    terms, crossed[1] = lax.optimization_barrier((terms, crossed[1]))
    terms = swap(terms.reshape(dev_count, tokens, width), "dev")
    terms, crossed[2] = lax.optimization_barrier((terms, crossed[2]))
    attended, outgoing, shares = route(
        terms, residual, norm_gain.reshape(1, width), router.T, expert_ids, node_count, cap
    )
    arrived = swap(outgoing.reshape(devices, cap, width // 2), ALL)
    served = experts(arrived.reshape(devices * cap, width // 2), finish(crossed), cap)
    returned = swap(served.reshape(devices, cap, width // 2), ALL)
    return attended, combine(shares, returned.reshape(devices * cap, width // 2))


def solution(mesh):
    placed = (
        P("node", "dev"),
        P("node", "dev"),
        P("node", None),
        P("node", None),
        P(ALL, None, None),
        P(ALL, None, None),
        P(),
        P("dev", None, None),
        P("dev", None, None),
        P("dev", None),
        P(ALL, None),
        P(),
        P(),
        P(ALL, None),
        P(ALL, None, None),
        P(ALL, None, None),
        P(ALL, None, None),
    )
    return jax.shard_map(
        on_device,
        mesh=mesh,
        in_specs=placed,
        out_specs=(P(ALL, None), P(ALL, None)),
        check_vma=False,
    )
```

```python
import functools
import math

import jax
import jax.numpy as jnp
from jax import lax
from jax.experimental import pallas as pl
from jax.experimental.pallas import tpu as pltpu
from jax.sharding import PartitionSpec as P

ROUTE_SCALE = 2.827
NORM_EPS = 1e-06
FAR_BELOW = -1e30
ALL = ("node", "dev")
VMEM_BYTES = 60 * 1024 * 1024
F32 = jnp.float32
BF16 = jnp.bfloat16


def dot(a, b, dims=(((1,), (0,)), ((), ()))):
    return lax.dot_general(a, b, dims, preferred_element_type=F32)


def swap(value, axis):
    return lax.all_to_all(value, axis, split_axis=0, concat_axis=0, tiled=True)


def fold(q_lat, q_rope, lat, rot, mask, old, new, scale):
    top, total, mixed = new
    heads, tokens = len(q_lat), q_rope.shape[0]
    rope = q_rope.shape[1] // heads
    for h in range(heads):
        rows = pl.ds(h * tokens, tokens)
        scores = dot(q_lat[h], lat, (((1,), (1,)), ((), ())))
        across = (((1,), (0,)), ((), ())) if rot.shape[0] == rope else (((1,), (1,)), ((), ()))
        scores = scores + dot(q_rope[:, h * rope : (h + 1) * rope], rot, across)
        if mask is not None:
            scores = jnp.where(mask, scores, FAR_BELOW)
        row_top = jnp.max(scores, axis=1, keepdims=True)
        if old is not None:
            old_top = old[0][rows]
            row_top = jnp.maximum(row_top, old_top)
        exp_scores = jnp.exp((scores - row_top) * scale)
        row_sum = jnp.sum(exp_scores, axis=1, keepdims=True)
        mix = dot(exp_scores.astype(BF16), lat)
        if old is not None:
            shrink = jnp.exp((old_top - row_top) * scale)
            row_sum = row_sum + old[1][rows] * shrink
            mix = mix + old[2][rows] * shrink
        top[rows] = row_top
        total[rows] = row_sum
        mixed[rows] = mix


def span_kernel(q_nope, q_rope, keys, absorb_k, q_lat, top, total, mixed, *, block):
    heads, nope, rank = absorb_k.shape
    tokens = q_nope.shape[0]
    rope = q_rope.shape[1] // heads
    span = block - rope
    scale = 1.0 / math.sqrt(nope + rope)
    node = lax.axis_index("node")
    first = pl.program_id(0) * tokens
    for h in range(heads):
        part = dot(q_nope[:, h * nope : (h + 1) * nope], absorb_k[h])
        q_lat[h * tokens : (h + 1) * tokens] = part.astype(BF16)

    def add(at, mask, old):
        q_parts = [q_lat[pl.ds(h * tokens, tokens)] for h in range(heads)]
        lat, rot = keys[pl.ds(at, span)], keys[pl.ds(at + span, rope)]
        fold(q_parts, q_rope, lat, rot, mask, old, (top, total, mixed), scale)

    q_pos = first + lax.broadcasted_iota(jnp.int32, (tokens, span), 0)
    key_pos = lax.broadcasted_iota(jnp.int32, (tokens, span), 1)
    add(pl.multiple_of(node * block, 64), key_pos <= q_pos, None)

    def earlier(j, carry):
        add(pl.multiple_of(j * block, 64), None, (top, total, mixed))
        return carry

    lax.fori_loop(0, node, earlier, 0)


def prefix_kernel(
    q_lat,
    q_rope,
    prefix,
    old_top,
    old_total,
    old_mixed,
    absorb_v,
    out_proj,
    terms,
    top,
    total,
    mixed,
    lat,
    *,
    scale,
):
    heads = absorb_v.shape[0]
    tokens = q_rope.shape[0]
    rope = q_rope.shape[1] // heads
    keys, rank = lat.shape
    for c in range(rank // 128):
        lat[:, c * 128 : (c + 1) * 128] = prefix[c * keys : (c + 1) * keys]
    rot = prefix[rank // 128 * keys : (rank // 128 + 1) * keys, :rope]
    q_parts = [q_lat[h * tokens : (h + 1) * tokens] for h in range(heads)]
    old = (old_top, old_total, old_mixed)
    fold(q_parts, q_rope, lat[...], rot, None, old, (top, total, mixed), scale)
    outs = []
    for h in range(heads):
        rows = pl.ds(h * tokens, tokens)
        head_lat = (mixed[rows] / total[rows]).astype(BF16)
        outs.append(dot(head_lat, absorb_v[h]).astype(BF16))
    head_out = jnp.concatenate(outs, axis=1)
    width = out_proj.shape[1]
    step = 512
    for c in range(0, width, step):
        terms[:, c : c + step] = dot(head_out, out_proj[:, c : c + step]).astype(BF16)


def attend_span(q_nope, q_rope, keys, absorb_k, block):
    rows = q_nope.shape[0]
    tile = min(256, rows)
    heads, nope, rank = absorb_k.shape
    whole = pl.BlockSpec(memory_space=pltpu.VMEM)
    state = [
        jax.ShapeDtypeStruct((heads * rows, rank), BF16),
        jax.ShapeDtypeStruct((heads * rows, 1), F32),
        jax.ShapeDtypeStruct((heads * rows, 1), F32),
        jax.ShapeDtypeStruct((heads * rows, rank), F32),
    ]
    pairs = heads * rows * keys.shape[0]
    return pl.pallas_call(
        functools.partial(span_kernel, block=block),
        grid=(rows // tile,),
        out_shape=state,
        in_specs=[
            pl.BlockSpec((tile, q_nope.shape[1]), lambda i: (i, 0)),
            pl.BlockSpec((tile, q_rope.shape[1]), lambda i: (i, 0)),
            whole,
            whole,
        ],
        out_specs=[pl.BlockSpec((heads * tile, s.shape[1]), lambda i: (i, 0)) for s in state],
        compiler_params=pltpu.CompilerParams(vmem_limit_bytes=VMEM_BYTES),
        cost_estimate=pl.CostEstimate(
            flops=2 * pairs * (2 * rank + 64), bytes_accessed=8 << 20, transcendentals=pairs
        ),
        name="attend_span",
    )(q_nope, q_rope, keys, absorb_k)


def attend_prefix(state, q_rope, prefix, absorb_v, out_proj, nope, keys):
    rows = q_rope.shape[0]
    tile = min(256, rows)
    heads, rank, _ = absorb_v.shape
    rope = q_rope.shape[1] // heads
    width = out_proj.shape[1]
    whole = pl.BlockSpec(memory_space=pltpu.VMEM)
    specs = [pl.BlockSpec((heads * tile, s.shape[1]), lambda i: (i, 0)) for s in state]
    return pl.pallas_call(
        functools.partial(prefix_kernel, scale=1.0 / math.sqrt(nope + rope)),
        grid=(rows // tile,),
        out_shape=jax.ShapeDtypeStruct((rows, width), BF16),
        in_specs=[
            specs[0],
            pl.BlockSpec((tile, q_rope.shape[1]), lambda i: (i, 0)),
            whole,
            specs[1],
            specs[2],
            specs[3],
            whole,
            whole,
        ],
        out_specs=pl.BlockSpec((tile, width), lambda i: (i, 0)),
        scratch_shapes=[
            pltpu.VMEM((heads * tile, 1), F32),
            pltpu.VMEM((heads * tile, 1), F32),
            pltpu.VMEM((heads * tile, rank), F32),
            pltpu.VMEM((keys, rank), BF16),
        ],
        compiler_params=pltpu.CompilerParams(vmem_limit_bytes=VMEM_BYTES),
        cost_estimate=pl.CostEstimate(flops=6 << 30, bytes_accessed=10 << 20, transcendentals=0),
        name="attend_prefix",
    )(state[0], q_rope, prefix, state[1], state[2], state[3], absorb_v, out_proj)


def slot_place(column, nodes, cap, experts):
    half = cap // 2
    devs = 2 * experts // nodes
    device, part, low = column // cap, column % cap // half, column % half
    node, dev = device // devs, device % devs
    expert = (experts // nodes) * (node // 2 * 2 + dev % 2) + dev // 2
    return expert, node % 2 * half + low, part


def route_kernel(terms, residual, gain, router, ids, attended, outgoing, shares, *, nodes, cap):
    groups, tokens, width = terms.shape
    experts = router.shape[0]
    top_k = ids.shape[1]
    acc = terms[0].astype(F32)
    for g in range(1, groups):
        acc = acc + terms[g].astype(F32)
    stream = (residual[...].astype(F32) + acc).astype(BF16)
    attended[...] = stream
    stream = stream.astype(F32)
    mean = jnp.mean(stream * stream, axis=1, keepdims=True)
    normed = (stream * lax.rsqrt(mean + NORM_EPS) * gain[...].astype(F32)).astype(BF16)
    logits = dot(normed, router[...], (((1,), (1,)), ((), ())))
    expert = lax.broadcasted_iota(jnp.int32, (tokens, experts), 1)
    hits = [ids[:, j : j + 1] == expert for j in range(top_k)]
    gates = [
        jax.nn.sigmoid(jnp.sum(jnp.where(hit, logits, 0.0), axis=1, keepdims=True)) for hit in hits
    ]
    gate_sum = functools.reduce(lambda a, b: a + b, gates)
    weight = jnp.zeros((tokens, experts), F32)
    used = jnp.zeros((tokens, experts), F32)
    for hit, gate in zip(hits, gates):
        weight = jnp.where(hit, ROUTE_SCALE * gate / gate_sum, weight)
        used = jnp.where(hit, 1.0, used)
    weight = weight.astype(BF16)
    used = used.astype(BF16)
    below = lax.broadcasted_iota(jnp.int32, (tokens, tokens), 1) < lax.broadcasted_iota(
        jnp.int32, (tokens, tokens), 0
    )
    rank = dot(below.astype(BF16), used).astype(BF16)
    rows = 2 * experts * cap
    owner = slot_place(lax.broadcasted_iota(jnp.int32, (experts, rows), 1), nodes, cap, experts)[0]
    spread = (owner == lax.broadcasted_iota(jnp.int32, (experts, rows), 0)).astype(BF16)
    _, slot, part = slot_place(
        lax.broadcasted_iota(jnp.int32, (tokens, rows), 1), nodes, cap, experts
    )
    filled = (dot(used, spread) > 0.5) & (dot(rank, spread) == slot.astype(F32))
    share = jnp.where(filled, dot(weight, spread), 0.0)
    filled = filled.astype(F32)
    share = [jnp.where(part == p, share, 0.0) for p in range(2)]
    filled = [jnp.where(part == p, filled, 0.0) for p in range(2)]
    shares[...] = jnp.concatenate(share, 0).astype(BF16)
    fill = jnp.concatenate(filled, 0).astype(BF16)
    narrow = width // 2
    halves = jnp.concatenate([normed[:, :narrow], normed[:, narrow:]], 0)
    step = narrow // 2
    for c in range(0, narrow, step):
        outgoing[:, c : c + step] = dot(
            fill, halves[:, c : c + step], (((0,), (0,)), ((), ()))
        ).astype(BF16)


def route(terms, residual, gain, router, ids, nodes, cap):
    tokens, width = residual.shape
    rows = 2 * router.shape[0] * cap
    whole = pl.BlockSpec(memory_space=pltpu.VMEM)
    return pl.pallas_call(
        functools.partial(route_kernel, nodes=nodes, cap=cap),
        out_shape=(
            jax.ShapeDtypeStruct((tokens, width), BF16),
            jax.ShapeDtypeStruct((rows, width // 2), BF16),
            jax.ShapeDtypeStruct((2 * tokens, rows), BF16),
        ),
        in_specs=[whole] * 5,
        out_specs=(whole, whole, whole),
        compiler_params=pltpu.CompilerParams(vmem_limit_bytes=VMEM_BYTES),
        name="route",
    )(terms, residual, gain, router, ids)


def expert_kernel(rows, *refs, cap):
    sources, (out, whole_rows, gates, ups, downs, sems) = refs[:14], refs[14:]
    node, dev = lax.axis_index("node"), lax.axis_index("dev")
    keeper = node % 2 == dev % 2
    own, crossed, twin, twin_crossed = sources[:3], sources[3:7], sources[7:10], sources[10:]
    slots = (gates, ups, downs)
    cut = ups.shape[1] // 2

    def copies(first, second):
        pieces = [(first[p].at[0], slots[p].at[0]) for p in range(3)]
        pieces.append((second[0].at[0], gates.at[1]))
        pieces.append((second[1].at[0], ups.at[1, pl.ds(0, cut)]))
        pieces.append((second[2].at[0], ups.at[1, pl.ds(cut, cut)]))
        pieces.append((second[3].at[0], downs.at[1]))
        return [
            pltpu.make_async_copy(here, there, sems.at[i]) for i, (here, there) in enumerate(pieces)
        ]

    order = (0, 1, 3, 4, 5, 2, 6)
    kept, given = copies(own, crossed), copies(twin, twin_crossed)

    @pl.when(keeper)
    def _():
        for i in order:
            kept[i].start()

    @pl.when(jnp.logical_not(keeper))
    def _():
        for i in order:
            given[i].start()

    count, narrow = rows.shape
    block = 256
    half = cap // 2
    here = lax.broadcasted_iota(jnp.int32, (block, block), 0)
    there = lax.broadcasted_iota(jnp.int32, (block, block), 1)
    mid = block // 2
    wanted = here % mid // half * cap + here // mid * half + here % half
    order_rows = (there == wanted).astype(F32).astype(BF16)
    for b in range(0, count, block):
        sorted_rows = dot(order_rows, rows[b : b + block]).astype(BF16)
        whole_rows[b // 2 : b // 2 + mid, :narrow] = sorted_rows[:mid]
        whole_rows[b // 2 : b // 2 + mid, narrow:] = sorted_rows[mid:]

    x = whole_rows[...]
    hidden = []
    for share in range(2):
        kept[3 * share].wait()
        gate_act = dot(x, gates[share])
        for i in ((1,), (4, 5))[share]:
            kept[i].wait()
        up_act = dot(x, ups[share])
        hidden.append((jax.nn.silu(gate_act) * up_act).astype(BF16))
    for i in (2, 6):
        kept[i].wait()
    step = narrow // 2
    for c in range(0, narrow, step):
        parts = []
        for at in (c, narrow + c):
            part = dot(hidden[0], downs[0, :, at : at + step])
            part = part + dot(hidden[1], downs[1, :, at : at + step])
            parts.append(part.astype(BF16))
        for b in range(0, count, block):
            both = jnp.concatenate([part[b // 2 : b // 2 + mid] for part in parts], 0)
            out[b : b + block, c : c + step] = dot(
                order_rows, both, (((0,), (0,)), ((), ()))
            ).astype(BF16)


def experts(rows, sources, cap):
    count, narrow = rows.shape
    _, width, hidden = sources[0].shape
    whole = pl.BlockSpec(memory_space=pltpu.VMEM)
    return pl.pallas_call(
        functools.partial(expert_kernel, cap=cap),
        out_shape=jax.ShapeDtypeStruct((count, narrow), BF16),
        in_specs=[whole] + [pl.BlockSpec(memory_space=pl.ANY)] * 14,
        out_specs=whole,
        scratch_shapes=[
            pltpu.VMEM((count // 2, width), BF16),
            pltpu.VMEM((2, width, hidden), BF16),
            pltpu.VMEM((2, width, hidden), BF16),
            pltpu.VMEM((2, hidden, width), BF16),
            pltpu.SemaphoreType.DMA((7,)),
        ],
        compiler_params=pltpu.CompilerParams(vmem_limit_bytes=VMEM_BYTES),
        name="experts",
    )(rows, *sources)


def placed_weights(weights, nodes, devs):
    across, beside = [], []
    for node in range(nodes):
        for dev in range(devs):
            if node % 2 == dev % 2:
                across.append((node * devs + (dev ^ 1), node * devs + dev))
            beside.append((node * devs + dev, (node ^ 1) * devs + dev))
    gate, up, down = weights
    cut = up.shape[1] // 2
    crossed = [lax.ppermute(w, ALL, across) for w in (gate, up[:, :cut], up[:, cut:])]

    def place_last(crossed, last):
        crossed = list(crossed) + [lax.ppermute(last, ALL, across)]
        twin = [lax.ppermute(w, ALL, beside) for w in weights]

        def finish(crossed):
            twin_crossed = [lax.ppermute(w, ALL, beside) for w in crossed]
            return list(weights) + list(crossed) + twin + twin_crossed

        return crossed, finish

    return crossed, place_last


def combine_kernel(shares, returned, out, total):
    tokens, width = out.shape
    part = dot(shares[...], returned[...])
    step = pl.program_id(0)

    @pl.when(step == 0)
    def _():
        total[...] = part

    @pl.when(step > 0)
    def _():
        total[...] += part

    @pl.when(step == pl.num_programs(0) - 1)
    def _():
        out[:, : width // 2] = total[:tokens].astype(BF16)
        out[:, width // 2 :] = total[tokens:].astype(BF16)


def combine(shares, returned):
    tokens, rows = shares.shape[0] // 2, shares.shape[1]
    narrow = returned.shape[1]
    tile = 256
    return pl.pallas_call(
        combine_kernel,
        grid=(rows // tile,),
        out_shape=jax.ShapeDtypeStruct((tokens, 2 * narrow), BF16),
        in_specs=[
            pl.BlockSpec((2 * tokens, tile), lambda i: (0, i)),
            pl.BlockSpec((tile, narrow), lambda i: (i, 0)),
        ],
        out_specs=pl.BlockSpec((tokens, 2 * narrow), lambda i: (0, 0)),
        scratch_shapes=[pltpu.VMEM((2 * tokens, narrow), F32)],
        compiler_params=pltpu.CompilerParams(vmem_limit_bytes=VMEM_BYTES),
        name="combine",
    )(shares, returned)


def listed_kernel(table, lat, rot, out):
    held, block, rank = lat.shape
    rope = rot.shape[2]
    count = table.shape[0]
    me = lax.axis_index("node") * lax.axis_size("dev") + lax.axis_index("dev")
    out[...] = jnp.zeros(out.shape, BF16)
    for b in range(count):
        entry = table[b]
        slot = entry % held

        @pl.when(entry // held == me)
        def _():
            for c in range(rank // 128):
                at = (c * count + b) * block
                out[at : at + block] = lat[slot, :, c * 128 : (c + 1) * 128]
            at = (rank // 128 * count + b) * block
            out[at : at + block, :rope] = rot[slot]


def spread_kernel(arrived, *refs):
    out = refs[-1]
    count = arrived.shape[0]
    piece = arrived[0].astype(F32)
    for d in range(1, count):
        piece = piece + arrived[d].astype(F32)
    out[...] = jnp.broadcast_to(piece.astype(BF16)[None], out.shape)


def listed_prefix(pool_latent, pool_rope, block_table, devices, first):
    held, block, rank = pool_latent.shape
    keys = block_table.shape[0] * block
    rows = -(-keys * (rank // 128 + 1) // (devices * 8)) * devices * 8
    whole = pl.BlockSpec(memory_space=pltpu.VMEM)
    mine = pl.pallas_call(
        listed_kernel,
        out_shape=jax.ShapeDtypeStruct((rows, 128), BF16),
        in_specs=[pl.BlockSpec(memory_space=pltpu.SMEM), whole, whole],
        out_specs=whole,
        compiler_params=pltpu.CompilerParams(vmem_limit_bytes=VMEM_BYTES),
        name="listed",
    )(block_table, pool_latent, pool_rope)
    arrived = swap(mine.reshape(devices, rows // devices, 128), ALL)
    state, crossed, last = first
    spread = pl.pallas_call(
        spread_kernel,
        out_shape=jax.ShapeDtypeStruct(arrived.shape, BF16),
        in_specs=[whole] + [pl.BlockSpec(memory_space=pl.ANY)] * len(state),
        out_specs=whole,
        compiler_params=pltpu.CompilerParams(vmem_limit_bytes=VMEM_BYTES),
        name="spread",
    )(arrived, *state)
    spread, crossed, last = lax.optimization_barrier((spread, crossed, last))
    return swap(spread, ALL).reshape(rows, 128), (state, crossed, last)


def on_device(
    q_nope,
    q_rope,
    kv_latent,
    k_rope,
    pool_latent,
    pool_rope,
    block_table,
    absorb_k,
    absorb_v,
    out_proj,
    residual,
    norm_gain,
    router,
    expert_ids,
    expert_gate,
    expert_up,
    expert_down,
):
    node_count = lax.axis_size("node")
    dev_count = lax.axis_size("dev")
    devices = node_count * dev_count
    prefix_keys = block_table.shape[0] * pool_latent.shape[1]
    tokens, width = residual.shape
    expert_count = router.shape[1]
    cap = max(2, 2 * tokens * expert_ids.shape[1] // expert_count)

    crossed, place_last = placed_weights(
        (expert_gate, expert_up, expert_down), node_count, dev_count
    )
    keys_here = jnp.concatenate([kv_latent, k_rope.T], 0)
    keys = lax.all_gather(keys_here, "node", axis=0, tiled=True)
    state = attend_span(q_nope, q_rope, keys, absorb_k, keys_here.shape[0])
    prefix, (state, crossed[:2], down) = listed_prefix(
        pool_latent, pool_rope, block_table, devices, (state, crossed[:2], expert_down)
    )
    crossed, finish = place_last(crossed, down)
    terms = attend_prefix(
        state, q_rope, prefix, absorb_v, out_proj, absorb_k.shape[1], prefix_keys
    )
    terms, crossed[:3] = lax.optimization_barrier((terms, crossed[:3]))
    terms = swap(terms.reshape(dev_count, tokens, width), "dev")
    terms, crossed[3] = lax.optimization_barrier((terms, crossed[3]))
    attended, outgoing, shares = route(
        terms, residual, norm_gain.reshape(1, width), router.T, expert_ids, node_count, cap
    )
    arrived = swap(outgoing.reshape(devices, cap, width // 2), ALL)
    served = experts(arrived.reshape(devices * cap, width // 2), finish(crossed), cap)
    returned = swap(served.reshape(devices, cap, width // 2), ALL)
    return attended, combine(shares, returned.reshape(devices * cap, width // 2))


def solution(mesh):
    placed = (
        P("node", "dev"),
        P("node", "dev"),
        P("node", None),
        P("node", None),
        P(ALL, None, None),
        P(ALL, None, None),
        P(),
        P("dev", None, None),
        P("dev", None, None),
        P("dev", None),
        P(ALL, None),
        P(),
        P(),
        P(ALL, None),
        P(ALL, None, None),
        P(ALL, None, None),
        P(ALL, None, None),
    )
    return jax.shard_map(
        on_device,
        mesh=mesh,
        in_specs=placed,
        out_specs=(P(ALL, None), P(ALL, None)),
        check_vma=False,
    )
```

```python
import functools
import math

import jax
import jax.numpy as jnp
from jax import lax
from jax.experimental import pallas as pl
from jax.experimental.pallas import tpu as pltpu
from jax.sharding import PartitionSpec as P

ROUTE_SCALE = 2.827
NORM_EPS = 1e-06
FAR_BELOW = -1e30
ALL = ("node", "dev")
VMEM_BYTES = 60 * 1024 * 1024
F32 = jnp.float32
BF16 = jnp.bfloat16


def dot(a, b, dims=(((1,), (0,)), ((), ()))):
    return lax.dot_general(a, b, dims, preferred_element_type=F32)


def swap(value, axis):
    return lax.all_to_all(value, axis, split_axis=0, concat_axis=0, tiled=True)


def fold(q_lat, q_rope, lat, rot, mask, old, new, scale):
    top, total, mixed = new
    heads, tokens = len(q_lat), q_rope.shape[0]
    rope = q_rope.shape[1] // heads
    for h in range(heads):
        rows = pl.ds(h * tokens, tokens)
        scores = dot(q_lat[h], lat, (((1,), (1,)), ((), ())))
        across = (((1,), (0,)), ((), ())) if rot.shape[0] == rope else (((1,), (1,)), ((), ()))
        scores = scores + dot(q_rope[:, h * rope : (h + 1) * rope], rot, across)
        if mask is not None:
            scores = jnp.where(mask, scores, FAR_BELOW)
        row_top = jnp.max(scores, axis=1, keepdims=True)
        if old is not None:
            old_top = old[0][rows]
            row_top = jnp.maximum(row_top, old_top)
        exp_scores = jnp.exp((scores - row_top) * scale)
        row_sum = jnp.sum(exp_scores, axis=1, keepdims=True)
        mix = dot(exp_scores.astype(BF16), lat)
        if old is not None:
            shrink = jnp.exp((old_top - row_top) * scale)
            row_sum = row_sum + old[1][rows] * shrink
            mix = mix + old[2][rows] * shrink
        top[rows] = row_top
        total[rows] = row_sum
        mixed[rows] = mix


def span_kernel(q_nope, q_rope, keys, absorb_k, q_lat, top, total, mixed, *, block):
    heads, nope, rank = absorb_k.shape
    tokens = q_nope.shape[0]
    rope = q_rope.shape[1] // heads
    span = block - rope
    scale = 1.0 / math.sqrt(nope + rope)
    node = lax.axis_index("node")
    first = pl.program_id(0) * tokens
    for h in range(heads):
        part = dot(q_nope[:, h * nope : (h + 1) * nope], absorb_k[h])
        q_lat[h * tokens : (h + 1) * tokens] = part.astype(BF16)

    def add(at, mask, old):
        q_parts = [q_lat[pl.ds(h * tokens, tokens)] for h in range(heads)]
        lat, rot = keys[pl.ds(at, span)], keys[pl.ds(at + span, rope)]
        fold(q_parts, q_rope, lat, rot, mask, old, (top, total, mixed), scale)

    q_pos = first + lax.broadcasted_iota(jnp.int32, (tokens, span), 0)
    key_pos = lax.broadcasted_iota(jnp.int32, (tokens, span), 1)
    add(pl.multiple_of(node * block, 64), key_pos <= q_pos, None)

    def earlier(j, carry):
        add(pl.multiple_of(j * block, 64), None, (top, total, mixed))
        return carry

    lax.fori_loop(0, node, earlier, 0)


def prefix_kernel(
    q_lat,
    q_rope,
    prefix,
    old_top,
    old_total,
    old_mixed,
    absorb_v,
    out_proj,
    terms,
    top,
    total,
    mixed,
    lat,
    *,
    scale,
):
    heads = absorb_v.shape[0]
    tokens = q_rope.shape[0]
    rope = q_rope.shape[1] // heads
    keys, rank = lat.shape
    for c in range(rank // 128):
        lat[:, c * 128 : (c + 1) * 128] = prefix[c * keys : (c + 1) * keys]
    rot = prefix[rank // 128 * keys : (rank // 128 + 1) * keys, :rope]
    q_parts = [q_lat[h * tokens : (h + 1) * tokens] for h in range(heads)]
    old = (old_top, old_total, old_mixed)
    fold(q_parts, q_rope, lat[...], rot, None, old, (top, total, mixed), scale)
    outs = []
    for h in range(heads):
        rows = pl.ds(h * tokens, tokens)
        head_lat = (mixed[rows] / total[rows]).astype(BF16)
        outs.append(dot(head_lat, absorb_v[h]).astype(BF16))
    head_out = jnp.concatenate(outs, axis=1)
    width = out_proj.shape[1]
    step = 512
    for c in range(0, width, step):
        terms[:, c : c + step] = dot(head_out, out_proj[:, c : c + step]).astype(BF16)


def attend_span(q_nope, q_rope, keys, absorb_k, block):
    rows = q_nope.shape[0]
    tile = min(256, rows)
    heads, nope, rank = absorb_k.shape
    whole = pl.BlockSpec(memory_space=pltpu.VMEM)
    state = [
        jax.ShapeDtypeStruct((heads * rows, rank), BF16),
        jax.ShapeDtypeStruct((heads * rows, 1), F32),
        jax.ShapeDtypeStruct((heads * rows, 1), F32),
        jax.ShapeDtypeStruct((heads * rows, rank), F32),
    ]
    pairs = heads * rows * keys.shape[0]
    return pl.pallas_call(
        functools.partial(span_kernel, block=block),
        grid=(rows // tile,),
        out_shape=state,
        in_specs=[
            pl.BlockSpec((tile, q_nope.shape[1]), lambda i: (i, 0)),
            pl.BlockSpec((tile, q_rope.shape[1]), lambda i: (i, 0)),
            whole,
            whole,
        ],
        out_specs=[pl.BlockSpec((heads * tile, s.shape[1]), lambda i: (i, 0)) for s in state],
        compiler_params=pltpu.CompilerParams(vmem_limit_bytes=VMEM_BYTES),
        cost_estimate=pl.CostEstimate(
            flops=2 * pairs * (2 * rank + 64), bytes_accessed=8 << 20, transcendentals=pairs
        ),
        name="attend_span",
    )(q_nope, q_rope, keys, absorb_k)


def attend_prefix(state, q_rope, prefix, absorb_v, out_proj, nope, keys):
    rows = q_rope.shape[0]
    tile = min(256, rows)
    heads, rank, _ = absorb_v.shape
    rope = q_rope.shape[1] // heads
    width = out_proj.shape[1]
    whole = pl.BlockSpec(memory_space=pltpu.VMEM)
    specs = [pl.BlockSpec((heads * tile, s.shape[1]), lambda i: (i, 0)) for s in state]
    return pl.pallas_call(
        functools.partial(prefix_kernel, scale=1.0 / math.sqrt(nope + rope)),
        grid=(rows // tile,),
        out_shape=jax.ShapeDtypeStruct((rows, width), BF16),
        in_specs=[
            specs[0],
            pl.BlockSpec((tile, q_rope.shape[1]), lambda i: (i, 0)),
            whole,
            specs[1],
            specs[2],
            specs[3],
            whole,
            whole,
        ],
        out_specs=pl.BlockSpec((tile, width), lambda i: (i, 0)),
        scratch_shapes=[
            pltpu.VMEM((heads * tile, 1), F32),
            pltpu.VMEM((heads * tile, 1), F32),
            pltpu.VMEM((heads * tile, rank), F32),
            pltpu.VMEM((keys, rank), BF16),
        ],
        compiler_params=pltpu.CompilerParams(vmem_limit_bytes=VMEM_BYTES),
        cost_estimate=pl.CostEstimate(flops=6 << 30, bytes_accessed=10 << 20, transcendentals=0),
        name="attend_prefix",
    )(state[0], q_rope, prefix, state[1], state[2], state[3], absorb_v, out_proj)


def slot_place(column, nodes, cap, experts):
    half = cap // 2
    devs = 2 * experts // nodes
    device, part, low = column // cap, column % cap // half, column % half
    node, dev = device // devs, device % devs
    expert = (experts // nodes) * (node // 2 * 2 + dev % 2) + dev // 2
    return expert, node % 2 * half + low, part


def route_kernel(terms, residual, gain, router, ids, attended, outgoing, shares, *, nodes, cap):
    groups, tokens, width = terms.shape
    experts = router.shape[0]
    top_k = ids.shape[1]
    acc = terms[0].astype(F32)
    for g in range(1, groups):
        acc = acc + terms[g].astype(F32)
    stream = (residual[...].astype(F32) + acc).astype(BF16)
    attended[...] = stream
    stream = stream.astype(F32)
    mean = jnp.mean(stream * stream, axis=1, keepdims=True)
    normed = (stream * lax.rsqrt(mean + NORM_EPS) * gain[...].astype(F32)).astype(BF16)
    logits = dot(normed, router[...], (((1,), (1,)), ((), ())))
    expert = lax.broadcasted_iota(jnp.int32, (tokens, experts), 1)
    hits = [ids[:, j : j + 1] == expert for j in range(top_k)]
    gates = [
        jax.nn.sigmoid(jnp.sum(jnp.where(hit, logits, 0.0), axis=1, keepdims=True)) for hit in hits
    ]
    gate_sum = functools.reduce(lambda a, b: a + b, gates)
    weight = jnp.zeros((tokens, experts), F32)
    used = jnp.zeros((tokens, experts), F32)
    for hit, gate in zip(hits, gates):
        weight = jnp.where(hit, ROUTE_SCALE * gate / gate_sum, weight)
        used = jnp.where(hit, 1.0, used)
    weight = weight.astype(BF16)
    used = used.astype(BF16)
    below = lax.broadcasted_iota(jnp.int32, (tokens, tokens), 1) < lax.broadcasted_iota(
        jnp.int32, (tokens, tokens), 0
    )
    rank = dot(below.astype(BF16), used).astype(BF16)
    rows = 2 * experts * cap
    owner = slot_place(lax.broadcasted_iota(jnp.int32, (experts, rows), 1), nodes, cap, experts)[0]
    spread = (owner == lax.broadcasted_iota(jnp.int32, (experts, rows), 0)).astype(BF16)
    _, slot, part = slot_place(
        lax.broadcasted_iota(jnp.int32, (tokens, rows), 1), nodes, cap, experts
    )
    filled = (dot(used, spread) > 0.5) & (dot(rank, spread) == slot.astype(F32))
    share = jnp.where(filled, dot(weight, spread), 0.0)
    filled = filled.astype(F32)
    share = [jnp.where(part == p, share, 0.0) for p in range(2)]
    filled = [jnp.where(part == p, filled, 0.0) for p in range(2)]
    shares[...] = jnp.concatenate(share, 0).astype(BF16)
    fill = jnp.concatenate(filled, 0).astype(BF16)
    narrow = width // 2
    halves = jnp.concatenate([normed[:, :narrow], normed[:, narrow:]], 0)
    step = narrow // 2
    for c in range(0, narrow, step):
        outgoing[:, c : c + step] = dot(
            fill, halves[:, c : c + step], (((0,), (0,)), ((), ()))
        ).astype(BF16)


def route(terms, residual, gain, router, ids, nodes, cap):
    tokens, width = residual.shape
    rows = 2 * router.shape[0] * cap
    whole = pl.BlockSpec(memory_space=pltpu.VMEM)
    return pl.pallas_call(
        functools.partial(route_kernel, nodes=nodes, cap=cap),
        out_shape=(
            jax.ShapeDtypeStruct((tokens, width), BF16),
            jax.ShapeDtypeStruct((rows, width // 2), BF16),
            jax.ShapeDtypeStruct((2 * tokens, rows), BF16),
        ),
        in_specs=[whole] * 5,
        out_specs=(whole, whole, whole),
        compiler_params=pltpu.CompilerParams(vmem_limit_bytes=VMEM_BYTES),
        name="route",
    )(terms, residual, gain, router, ids)


def expert_kernel(rows, *refs, cap):
    sources, (out, whole_rows, gates, ups, downs, sems) = refs[:14], refs[14:]
    node, dev = lax.axis_index("node"), lax.axis_index("dev")
    keeper = node % 2 == dev % 2
    own, crossed, twin, twin_crossed = sources[:3], sources[3:7], sources[7:10], sources[10:]
    slots = (gates, ups, downs)
    cut = ups.shape[1] // 2

    def copies(first, second):
        pieces = [(first[p].at[0], slots[p].at[0]) for p in range(3)]
        pieces.append((second[0].at[0], gates.at[1]))
        pieces.append((second[1].at[0], ups.at[1, pl.ds(0, cut)]))
        pieces.append((second[2].at[0], ups.at[1, pl.ds(cut, cut)]))
        pieces.append((second[3].at[0], downs.at[1]))
        return [
            pltpu.make_async_copy(here, there, sems.at[i]) for i, (here, there) in enumerate(pieces)
        ]

    order = (0, 1, 3, 4, 5, 2, 6)
    kept, given = copies(own, crossed), copies(twin, twin_crossed)

    @pl.when(keeper)
    def _():
        for i in order:
            kept[i].start()

    @pl.when(jnp.logical_not(keeper))
    def _():
        for i in order:
            given[i].start()

    count, narrow = rows.shape
    block = 256
    half = cap // 2
    here = lax.broadcasted_iota(jnp.int32, (block, block), 0)
    there = lax.broadcasted_iota(jnp.int32, (block, block), 1)
    mid = block // 2
    wanted = here % mid // half * cap + here // mid * half + here % half
    order_rows = (there == wanted).astype(F32).astype(BF16)
    wanted = there % mid // half * cap + there // mid * half + there % half
    order_back = (here == wanted).astype(F32).astype(BF16)
    for b in range(0, count, block):
        sorted_rows = dot(order_rows, rows[b : b + block]).astype(BF16)
        whole_rows[b // 2 : b // 2 + mid, :narrow] = sorted_rows[:mid]
        whole_rows[b // 2 : b // 2 + mid, narrow:] = sorted_rows[mid:]

    x = whole_rows[...]
    hidden = []
    for share in range(2):
        kept[3 * share].wait()
        gate_act = dot(x, gates[share])
        for i in ((1,), (4, 5))[share]:
            kept[i].wait()
        up_act = dot(x, ups[share])
        hidden.append((jax.nn.silu(gate_act) * up_act).astype(BF16))
    for i in (2, 6):
        kept[i].wait()
    step = narrow // 2
    for c in range(0, narrow, step):
        parts = []
        for at in (c, narrow + c):
            part = dot(hidden[0], downs[0, :, at : at + step])
            part = part + dot(hidden[1], downs[1, :, at : at + step])
            parts.append(part.astype(BF16))
        for b in range(0, count, block):
            both = jnp.concatenate([part[b // 2 : b // 2 + mid] for part in parts], 0)
            out[b : b + block, c : c + step] = dot(order_back, both).astype(BF16)


def experts(rows, sources, cap):
    count, narrow = rows.shape
    _, width, hidden = sources[0].shape
    whole = pl.BlockSpec(memory_space=pltpu.VMEM)
    return pl.pallas_call(
        functools.partial(expert_kernel, cap=cap),
        out_shape=jax.ShapeDtypeStruct((count, narrow), BF16),
        in_specs=[whole] + [pl.BlockSpec(memory_space=pl.ANY)] * 14,
        out_specs=whole,
        scratch_shapes=[
            pltpu.VMEM((count // 2, width), BF16),
            pltpu.VMEM((2, width, hidden), BF16),
            pltpu.VMEM((2, width, hidden), BF16),
            pltpu.VMEM((2, hidden, width), BF16),
            pltpu.SemaphoreType.DMA((7,)),
        ],
        compiler_params=pltpu.CompilerParams(vmem_limit_bytes=VMEM_BYTES),
        name="experts",
    )(rows, *sources)


def placed_weights(weights, nodes, devs):
    across, beside = [], []
    for node in range(nodes):
        for dev in range(devs):
            if node % 2 == dev % 2:
                across.append((node * devs + (dev ^ 1), node * devs + dev))
            beside.append((node * devs + dev, (node ^ 1) * devs + dev))
    gate, up, down = weights
    cut = up.shape[1] // 2
    crossed = [lax.ppermute(w, ALL, across) for w in (gate, up[:, :cut], up[:, cut:])]

    def place_last(crossed, last):
        crossed = list(crossed) + [lax.ppermute(last, ALL, across)]
        twin = [lax.ppermute(w, ALL, beside) for w in weights]

        def finish(crossed):
            twin_crossed = [lax.ppermute(w, ALL, beside) for w in crossed]
            return list(weights) + list(crossed) + twin + twin_crossed

        return crossed, finish

    return crossed, place_last


def combine_kernel(shares, returned, out, total):
    tokens, width = out.shape
    part = dot(shares[...], returned[...])
    step = pl.program_id(0)

    @pl.when(step == 0)
    def _():
        total[...] = part

    @pl.when(step > 0)
    def _():
        total[...] += part

    @pl.when(step == pl.num_programs(0) - 1)
    def _():
        out[:, : width // 2] = total[:tokens].astype(BF16)
        out[:, width // 2 :] = total[tokens:].astype(BF16)


def combine(shares, returned):
    tokens, rows = shares.shape[0] // 2, shares.shape[1]
    narrow = returned.shape[1]
    tile = 256
    return pl.pallas_call(
        combine_kernel,
        grid=(rows // tile,),
        out_shape=jax.ShapeDtypeStruct((tokens, 2 * narrow), BF16),
        in_specs=[
            pl.BlockSpec((2 * tokens, tile), lambda i: (0, i)),
            pl.BlockSpec((tile, narrow), lambda i: (i, 0)),
        ],
        out_specs=pl.BlockSpec((tokens, 2 * narrow), lambda i: (0, 0)),
        scratch_shapes=[pltpu.VMEM((2 * tokens, narrow), F32)],
        compiler_params=pltpu.CompilerParams(vmem_limit_bytes=VMEM_BYTES),
        name="combine",
    )(shares, returned)


def listed_kernel(table, lat, rot, out):
    held, block, rank = lat.shape
    rope = rot.shape[2]
    count = table.shape[0]
    me = lax.axis_index("node") * lax.axis_size("dev") + lax.axis_index("dev")
    out[...] = jnp.zeros(out.shape, BF16)
    for b in range(count):
        entry = table[b]
        slot = entry % held

        @pl.when(entry // held == me)
        def _():
            for c in range(rank // 128):
                at = (c * count + b) * block
                out[at : at + block] = lat[slot, :, c * 128 : (c + 1) * 128]
            at = (rank // 128 * count + b) * block
            out[at : at + block, :rope] = rot[slot]


def spread_kernel(arrived, *refs):
    out = refs[-1]
    count = arrived.shape[0]
    piece = arrived[0].astype(F32)
    for d in range(1, count):
        piece = piece + arrived[d].astype(F32)
    out[...] = jnp.broadcast_to(piece.astype(BF16)[None], out.shape)


def listed_prefix(pool_latent, pool_rope, block_table, devices, first):
    held, block, rank = pool_latent.shape
    keys = block_table.shape[0] * block
    rows = -(-keys * (rank // 128 + 1) // (devices * 8)) * devices * 8
    whole = pl.BlockSpec(memory_space=pltpu.VMEM)
    mine = pl.pallas_call(
        listed_kernel,
        out_shape=jax.ShapeDtypeStruct((rows, 128), BF16),
        in_specs=[pl.BlockSpec(memory_space=pltpu.SMEM), whole, whole],
        out_specs=whole,
        compiler_params=pltpu.CompilerParams(vmem_limit_bytes=VMEM_BYTES),
        name="listed",
    )(block_table, pool_latent, pool_rope)
    arrived = swap(mine.reshape(devices, rows // devices, 128), ALL)
    state, crossed, last = first
    spread = pl.pallas_call(
        spread_kernel,
        out_shape=jax.ShapeDtypeStruct(arrived.shape, BF16),
        in_specs=[whole] + [pl.BlockSpec(memory_space=pl.ANY)] * len(state),
        out_specs=whole,
        compiler_params=pltpu.CompilerParams(vmem_limit_bytes=VMEM_BYTES),
        name="spread",
    )(arrived, *state)
    spread, crossed, last = lax.optimization_barrier((spread, crossed, last))
    return swap(spread, ALL).reshape(rows, 128), (state, crossed, last)


def on_device(
    q_nope,
    q_rope,
    kv_latent,
    k_rope,
    pool_latent,
    pool_rope,
    block_table,
    absorb_k,
    absorb_v,
    out_proj,
    residual,
    norm_gain,
    router,
    expert_ids,
    expert_gate,
    expert_up,
    expert_down,
):
    node_count = lax.axis_size("node")
    dev_count = lax.axis_size("dev")
    devices = node_count * dev_count
    prefix_keys = block_table.shape[0] * pool_latent.shape[1]
    tokens, width = residual.shape
    expert_count = router.shape[1]
    cap = max(2, 2 * tokens * expert_ids.shape[1] // expert_count)

    crossed, place_last = placed_weights(
        (expert_gate, expert_up, expert_down), node_count, dev_count
    )
    keys_here = jnp.concatenate([kv_latent, k_rope.T], 0)
    keys = lax.all_gather(keys_here, "node", axis=0, tiled=True)
    state = attend_span(q_nope, q_rope, keys, absorb_k, keys_here.shape[0])
    prefix, (state, crossed[:2], down) = listed_prefix(
        pool_latent, pool_rope, block_table, devices, (state, crossed[:2], expert_down)
    )
    crossed, finish = place_last(crossed, down)
    terms = attend_prefix(
        state, q_rope, prefix, absorb_v, out_proj, absorb_k.shape[1], prefix_keys
    )
    terms, crossed[:3] = lax.optimization_barrier((terms, crossed[:3]))
    terms = swap(terms.reshape(dev_count, tokens, width), "dev")
    terms, crossed[3] = lax.optimization_barrier((terms, crossed[3]))
    attended, outgoing, shares = route(
        terms, residual, norm_gain.reshape(1, width), router.T, expert_ids, node_count, cap
    )
    arrived = swap(outgoing.reshape(devices, cap, width // 2), ALL)
    served = experts(arrived.reshape(devices * cap, width // 2), finish(crossed), cap)
    returned = swap(served.reshape(devices, cap, width // 2), ALL)
    return attended, combine(shares, returned.reshape(devices * cap, width // 2))


def solution(mesh):
    placed = (
        P("node", "dev"),
        P("node", "dev"),
        P("node", None),
        P("node", None),
        P(ALL, None, None),
        P(ALL, None, None),
        P(),
        P("dev", None, None),
        P("dev", None, None),
        P("dev", None),
        P(ALL, None),
        P(),
        P(),
        P(ALL, None),
        P(ALL, None, None),
        P(ALL, None, None),
        P(ALL, None, None),
    )
    return jax.shard_map(
        on_device,
        mesh=mesh,
        in_specs=placed,
        out_specs=(P(ALL, None), P(ALL, None)),
        check_vma=False,
    )
```
